256 devices in a mesh: dp: 8 (over x, core), expert: 32 (over y, z).
Axes of the slice: x: 4, y: 4, z: 8, core: 2. Of those that a mesh axis runs over, the one named last changes fastest.
Arguments:
- output_gradient: bfloat16 [8, 4096, 4096], P('dp', 'expert'), may hold values from -6 to 6
- route_gate_weight: float32 [8, 4096, 8], P('dp', 'expert'), may hold values from 0.02 to 0.25
- routes: int32 [8, 4096, 8], P('dp', 'expert'), may hold values from 0 to 127, all different within a row; in each aligned block of 128 rows (0 to 127, 128 to 255, ..., all dimensions but the last counted through in order) at most 12 rows name the same one
- token_example: int32 [8, 4096], P('dp', 'expert'), may hold values from 0 to 15, never falling along the last dimension, each value on 1 to 512 neighbouring positions
- stored_hidden_slots: bfloat16 [8, 128, 384, 1536], P('dp', 'expert'), may hold values from -4 to 4
- adapter_down_weight: bfloat16 [128, 16, 1536], P('expert'), may hold values from -0.15625 to 0.15625
- adapter_up_weight: bfloat16 [128, 16, 4096], P('expert'), may hold values from -1.5 to 1.5
Outputs:
- hidden_grad: bfloat16 [8, 128, 384, 1536], P('dp', 'expert')
- grad_a: float32 [128, 16, 1536], P('expert', None, 'dp')
- grad_b: float32 [128, 16, 4096], P('expert', None, 'dp')
The draws below stay inside these ranges and needn't reach their ends.
Inputs may be any that keep to these rules, and one draw needn't show every extreme that they name: Among the routes of one device's 128 tokens, no expert is named by more than 12 routes, a bound that some block reaches. `token_example`: within a data group the example ids never fall along the tokens; every example has 1 to 512 tokens, and one has exactly that many.
All inputs are finite; a program needn't handle non-finite values.
Results may differ from the reference program's by a relative error of at most 0.0057.
Values may be sent and summed in bfloat16 or wider, within the bound.
No kernel may reach another device: no remote copies, remote signals or barrier semaphores. Data moves between devices by JAX's collectives and lax.ppermute only.
A program may use at most 128 MiB of HBM per device.

```python
import math
import jax
import jax.numpy as jnp
import numpy as np
from jax import lax

MODEL_WIDTH = 4096
HIDDEN_UNITS = 1536
ADAPTER_RANK = 16
TOPK = 8
TOK_DEV = 128
GROUP_EXAMPLES = 16
EXPERT_TOTAL = 128
DPG = 8
GROUP_TOK = 4096
CAP = 12
SLOTS = 384
N_EXPERT = 32


def block_levels(key, shape, shards, low, high):
    loudness = 1.0
    for dim, shards_of in shards:
        draws = jax.random.uniform(jax.random.fold_in(jax.random.fold_in(key, 6), dim), (shards_of,), jnp.float32, low / len(shards), high / len(shards))
        loudness = loudness * jnp.repeat(jnp.exp(draws), shape[dim] // shards_of).reshape((-1,) + (1,) * (len(shape) - 1 - dim))
    return loudness


def length_profile(count, total, reach, skew):
    loads = [(1 << 20) // math.isqrt(grade ** skew) + 1 for grade in range(2, count + 1)]
    surplus, counts = total - reach - (count - 1), [1] * (count - 1)
    while surplus > 0:
        movable = [i for i in range(count - 1) if counts[i] < reach]
        mass, budget = sum([loads[i] for i in movable]), surplus
        for i in movable:
            extra = min(reach - counts[i], max(1, budget * loads[i] // mass), surplus)
            counts[i] = counts[i] + extra
            surplus = surplus - extra
    return np.array([reach] + counts)


def uneven(key, count, total, limit, slope):
    if count == 2:
        one = jax.random.randint(key, (), max(1, total - limit), min(limit, total - 1) + 1)
        return jnp.stack([one, total - one])
    lengths = jnp.asarray(length_profile(count, total, limit, slope), jnp.int32)
    twos = (count - 1) // 2
    source_of, taker = lengths[1:1 + 2 * twos:2], lengths[2:2 + 2 * twos:2]
    margin = jnp.minimum(source_of - 1, limit - taker)
    moved = jax.random.randint(jax.random.fold_in(key, 1), (twos,), 0, 1 << 20) % (margin + 1)
    lengths = lengths.at[1:1 + 2 * twos:2].set(source_of - moved).at[2:2 + 2 * twos:2].set(taker + moved)
    return lengths[jax.random.permutation(jax.random.fold_in(key, 2), count)]


def routed_block(rng, own, number, rows, number_of, top, limit, slope):
    order = jax.random.permutation(rng, number_of)
    packed, ordinary = shares(number_of, rows * top, limit, slope, True), shares(number_of, rows * top, limit, slope, False)
    places = jnp.arange(number_of)

    def named(lengths, offset_by):
        used = int((lengths > 0).sum())
        fixed = max(1, used // 4)
        shifted = fixed + (places - fixed + offset_by * (used - fixed)) % max(1, number_of - fixed)
        return jnp.zeros((number_of,), jnp.int32).at[order[jnp.where(places < fixed, places, shifted)]].set(jnp.asarray(lengths, jnp.int32))

    lengths = jnp.where(number % 4 == 0, named(packed, number // 4), named(ordinary, number - number // 4 - 1))
    mixed = jax.random.permutation(jax.random.fold_in(own, 3), number_of)
    giver, sink = mixed[0:number_of // 2 * 2:2], mixed[1:number_of // 2 * 2:2]
    slack = jnp.minimum(lengths[giver] - 1, limit - lengths[sink]) // 2
    slack = jnp.where((giver == order[0]) | (sink == order[0]) | (lengths[sink] == 0), 0, jnp.maximum(slack, 0))
    shifted = jax.random.randint(jax.random.fold_in(own, 4), (number_of // 2,), 0, 1 << 20) % (slack + 1)
    lengths = lengths.at[giver].add(-shifted).at[sink].add(shifted)
    members = jnp.searchsorted(jnp.cumsum(lengths), jnp.arange(rows * top), side="right").astype(jnp.int32)
    table = members.reshape(top, rows).T
    table = table[jax.random.permutation(jax.random.fold_in(own, 1), rows)]
    offset_by = jax.random.randint(jax.random.fold_in(own, 2), (rows, 1), 0, top)
    return jnp.take_along_axis(table, (jnp.arange(top)[None, :] + offset_by) % top, axis=1)


def shares(count, total, most, lean, full):
    portions = [(1 << 20) // math.isqrt(grade ** lean) + 1 for grade in range(1, count + 1)]
    largest = most if full else min(most, max(-(-total // count), total * portions[0] // sum(portions)))
    least = 1 if total - largest >= count - 1 else 0
    given, rest = [largest] + [least] * (count - 1), total - largest - least * (count - 1)
    while rest > 0:
        free = [i for i in range(1, count) if given[i] < largest] or [i for i in range(1, count) if given[i] < most]
        mass, remaining = sum([portions[i] for i in free]), rest
        for i in free:
            extra = min(most - given[i], max(1, remaining * portions[i] // mass), rest)
            given[i] = given[i] + extra
            rest = rest - extra
    return np.array(given)


def normal_values(own_key, dims, spread, limit, split=(), kind=jnp.bfloat16):
    values = jax.random.normal(own_key, dims, jnp.float32) * spread
    if len(split) > 0:
        values = block_levels(own_key, dims, split, -0.22, 0.18) * values
    return jnp.clip(values, min=-limit, max=limit).astype(kind)


def setup_inputs(seed: int = 0) -> dict:
    key_list = jax.random.split(jax.random.key(seed), 8)
    output_gradient = normal_values(key_list[0], (DPG, GROUP_TOK, MODEL_WIDTH), 1.0, 6.0, ((0, 8), (1, 32)))
    route_gate_weight = jnp.clip(0.02 + 0.23 * jax.random.uniform(key_list[1], (DPG, GROUP_TOK, TOPK), jnp.float32) ** block_levels(key_list[1], (DPG, GROUP_TOK, TOPK), ((0, 8), (1, 32)), -0.2, 0.2), 0.02, 0.25)
    routes_keys = jax.random.split(jax.random.fold_in(key_list[2], 1), DPG * GROUP_TOK // TOK_DEV)
    routes_turns = jax.random.permutation(jax.random.fold_in(key_list[2], 3), DPG * GROUP_TOK // TOK_DEV)
    routes = jax.vmap(lambda own, number: routed_block(jax.random.fold_in(key_list[2], 2), own, number, TOK_DEV, EXPERT_TOTAL, TOPK, CAP, 2))(routes_keys, routes_turns).reshape((DPG, GROUP_TOK, TOPK))
    token_example = jax.vmap(lambda own: jnp.searchsorted(jnp.cumsum(uneven(own, GROUP_EXAMPLES, GROUP_TOK, 2 * GROUP_TOK // GROUP_EXAMPLES, 1)), jnp.arange(GROUP_TOK), side="right"))(jax.random.split(key_list[3], DPG)).reshape((DPG, GROUP_TOK)).astype(jnp.int32)
    stored_hidden_slots = normal_values(key_list[4], (DPG, EXPERT_TOTAL, SLOTS, HIDDEN_UNITS), 0.5, 4.0, ((0, 8), (1, 32)))
    adapter_down_weight = normal_values(key_list[5], (EXPERT_TOTAL, ADAPTER_RANK, HIDDEN_UNITS), HIDDEN_UNITS ** -0.5, 0.15625, ((0, 32),))
    adapter_up_weight = normal_values(key_list[6], (EXPERT_TOTAL, ADAPTER_RANK, MODEL_WIDTH), ADAPTER_RANK ** -0.5, 1.5, ((0, 32),))
    return {"output_gradient": output_gradient, "route_gate_weight": route_gate_weight, "routes": routes, "token_example": token_example, "stored_hidden_slots": stored_hidden_slots, "adapter_down_weight": adapter_down_weight, "adapter_up_weight": adapter_up_weight}


ADAPTER_SCALE = 2.0
CLIP_GAMMA = 0.01

def route_slots(routes_group):
    flat = routes_group.reshape(N_EXPERT, TOK_DEV * TOPK)
    matches = (flat[:, :, None] == jnp.arange(EXPERT_TOTAL, dtype=jnp.int32)[None, None, :]).astype(jnp.int32)
    rank_in = lax.optimization_barrier(jnp.sum(jnp.cumsum(matches, axis=1) * matches, axis=2)) - 1
    slot_of = jnp.arange(N_EXPERT, dtype=jnp.int32)[:, None] * CAP + rank_in
    return (flat.reshape(-1), slot_of.reshape(-1).astype(jnp.int32))

def per_expert_norm(operands):
    received_rows, target_labels, hidden_state, down_matrix, up_factor = operands
    lowrank_product = jnp.dot(hidden_state, down_matrix.T, preferred_element_type=jnp.float32).astype(jnp.bfloat16)
    backward_rank = jnp.dot(received_rows, up_factor.T, preferred_element_type=jnp.float32).astype(jnp.bfloat16)
    hidden_gradient = (ADAPTER_SCALE * jnp.dot(backward_rank, down_matrix, preferred_element_type=jnp.float32)).astype(jnp.bfloat16)
    member = (target_labels[:, None] == jnp.arange(GROUP_EXAMPLES, dtype=jnp.int32)[None, :]).astype(jnp.bfloat16)
    low_ex = (member[:, :, None] * lowrank_product[:, None, :]).reshape(-1, GROUP_EXAMPLES * ADAPTER_RANK)
    back_ex = (member[:, :, None] * backward_rank[:, None, :]).reshape(-1, GROUP_EXAMPLES * ADAPTER_RANK)
    stack_b = lax.dot_general(low_ex, received_rows, (((0,), (0,)), ((), ())), preferred_element_type=jnp.float32)
    stack_a = lax.dot_general(back_ex, hidden_state, (((0,), (0,)), ((), ())), preferred_element_type=jnp.float32)
    squared_norms = lax.optimization_barrier(jnp.sum(stack_b * stack_b, axis=1)) + lax.optimization_barrier(jnp.sum(stack_a * stack_a, axis=1))
    partial_result = ADAPTER_SCALE * ADAPTER_SCALE * lax.optimization_barrier(jnp.sum(squared_norms.reshape(GROUP_EXAMPLES, ADAPTER_RANK), axis=1))
    return (hidden_gradient, partial_result, lowrank_product, backward_rank)

def expert_grads(operands):
    received_rows, target_labels, hidden_state, lowrank_product, backward_rank, factor = operands
    member = (target_labels[:, None] == jnp.arange(GROUP_EXAMPLES, dtype=jnp.int32)[None, :]).astype(jnp.float32)
    weight = lax.optimization_barrier(jnp.sum(member * factor[None, :], axis=1))
    clipped_lowrank = (lowrank_product.astype(jnp.float32) * weight[:, None]).astype(jnp.bfloat16)
    clipped_backward = (backward_rank.astype(jnp.float32) * weight[:, None]).astype(jnp.bfloat16)
    partial_up = ADAPTER_SCALE * jnp.dot(clipped_lowrank.T, received_rows, preferred_element_type=jnp.float32)
    partial_down = ADAPTER_SCALE * jnp.dot(clipped_backward.T, hidden_state, preferred_element_type=jnp.float32)
    return (partial_down, partial_up)

def reference(output_gradient, route_gate_weight, routes, token_example, stored_hidden_slots, adapter_down_weight, adapter_up_weight):
    radius = math.sqrt(EXPERT_TOTAL * ADAPTER_RANK * (MODEL_WIDTH + HIDDEN_UNITS) / (DPG * GROUP_EXAMPLES))
    total_a = jnp.zeros((EXPERT_TOTAL, ADAPTER_RANK, HIDDEN_UNITS), jnp.float32)
    total_b = jnp.zeros((EXPERT_TOTAL, ADAPTER_RANK, MODEL_WIDTH), jnp.float32)
    hidden_parts = []
    for group_index in range(DPG):
        expert_of, slot_of = route_slots(routes[group_index])
        scaled = (route_gate_weight[group_index][:, :, None] * output_gradient[group_index][:, None, :].astype(jnp.float32)).astype(jnp.bfloat16)
        received_rows = jnp.zeros((EXPERT_TOTAL, SLOTS, MODEL_WIDTH), jnp.bfloat16).at[expert_of, slot_of].set(scaled.reshape(-1, MODEL_WIDTH))
        target_labels = jnp.full((EXPERT_TOTAL, SLOTS), -1, jnp.int32).at[expert_of, slot_of].set(jnp.repeat(token_example[group_index], TOPK))
        hidden_state = stored_hidden_slots[group_index]
        hidden_gradient, partial_result, lowrank_product, backward_rank = lax.map(per_expert_norm, (received_rows, target_labels, hidden_state, adapter_down_weight, adapter_up_weight))
        norm_sq = lax.optimization_barrier(jnp.sum(partial_result, axis=0))
        factor = radius / (jnp.sqrt(norm_sq) + CLIP_GAMMA)
        factors = jnp.broadcast_to(factor[None, :], (EXPERT_TOTAL, GROUP_EXAMPLES))
        partial_down, partial_up = lax.map(expert_grads, (received_rows, target_labels, hidden_state, lowrank_product, backward_rank, factors))
        total_a = total_a + partial_down
        total_b = total_b + partial_up
        hidden_parts.append(hidden_gradient)
    return (jnp.stack(hidden_parts, axis=0), total_a, total_b)
```

```python
import math

import jax
import jax.numpy as jnp
from jax import lax
from jax.experimental import pallas as pl
from jax.experimental.pallas import tpu as pltpu
from jax.sharding import PartitionSpec as P

NY, NZ, DP = 4, 8, 8
NSRC = NY * NZ
TOK = 128
TOPK = 8
D = 4096
DZ = D // NZ
F = 1536
R = 16
EXP = 128
EO = 4
EY = EXP // NY
CAP = 12
PCAP = 16
SLOTS = NSRC * CAP
PSLOTS = NSRC * PCAP
NEX = 16
MROWS = TOK + 16
SCALE = 2.0
GAMMA = 0.01
FA = F // DP
f32 = jnp.float32
bf16 = jnp.bfloat16
i32 = jnp.int32

ZGROUPS = [[y * NZ + z for z in range(NZ)] for y in range(NY)]
VMEM = pl.BlockSpec(memory_space=pltpu.VMEM)
SMEM = pl.BlockSpec(memory_space=pltpu.SMEM)
PARAMS = dict(vmem_limit_bytes=56 * 1024 * 1024)


def dot(a, b, ca=1, cb=0):
    return lax.dot_general(a, b, (((ca,), (cb,)), ((), ())), preferred_element_type=f32)


def iota(shape, dim):
    return lax.broadcasted_iota(i32, shape, dim)


def pad_matrix():
    lane = iota((SLOTS, PSLOTS), 1)
    s = lane & (PCAP - 1)
    at = (lane >> 4) * CAP + s
    return jnp.where((at == iota((SLOTS, PSLOTS), 0)) & (s < CAP), 1.0, 0.0).astype(bf16)


def send_kernel(x_ref, gate_ref, route_ref, example_ref, out_ref):
    expert = iota((TOK, EXP), 1)
    routed = jnp.zeros((TOK, EXP), f32)
    gate = jnp.zeros((TOK, EXP), f32)
    for k in range(TOPK):
        hit = route_ref[:, k : k + 1] == expert
        routed = jnp.where(hit, 1.0, routed)
        gate = jnp.where(hit, gate_ref[:, k : k + 1], gate)
    before = jnp.where(iota((TOK, TOK), 1) < iota((TOK, TOK), 0), 1.0, 0.0).astype(bf16)
    rank = jnp.where(routed > 0.5, dot(before, routed.astype(bf16)), 64.0).astype(bf16)
    high = gate.astype(bf16)
    low = (gate - high.astype(f32)).astype(bf16)
    row = iota((16, TOK), 0)
    ids = jnp.where(
        row == 0,
        iota((16, TOK), 1) + 1,
        jnp.where(row == 1, jnp.broadcast_to(example_ref[...], (16, TOK)) + 1, 0),
    ).astype(f32).astype(bf16)
    ones = jnp.ones((16, TOK), bf16)
    toks, highs, lows, labels = [], [], [], []
    for y in range(NY):
        lane = iota((EXP, EY * PCAP), 1)
        expand = jnp.where((lane >> 4) + y * EY == iota((EXP, EY * PCAP), 0), 1.0, 0.0).astype(bf16)
        place = (iota((TOK, EY * PCAP), 1) & (PCAP - 1)).astype(f32)
        here = dot(rank, expand) == place
        tab = dot(ids, jnp.where(here, 1.0, 0.0).astype(bf16))
        toks.append(tab[0:1])
        labels.append(tab[1:2])
        highs.append(dot(ones, jnp.where(here, dot(high, expand), 0.0).astype(bf16))[0:1])
        lows.append(dot(ones, jnp.where(here, dot(low, expand), 0.0).astype(bf16))[0:1])
    table = jnp.concatenate(toks + highs + lows + labels, axis=0).astype(bf16)
    for z in range(NZ):
        out_ref[z, 0:TOK, :] = x_ref[:, z * DZ : (z + 1) * DZ]
        out_ref[z, TOK:MROWS, :] = table


def low_kernel(hidden_ref, down_ref, up_ref, out_ref):
    j = pl.program_id(0)
    low = dot(down_ref[0], hidden_ref[0], 1, 1).astype(bf16)
    low = dot(low, pad_matrix()).astype(bf16)
    at = pl.multiple_of(j * R, R)
    for z in range(NZ):
        out_ref[z, pl.ds(at, R), :] = up_ref[0, :, z * DZ : (z + 1) * DZ]
        out_ref[z, pl.ds(EO * R + at, R), :] = low


def gather_rows(y, own, left, right, far0, far1, rows_ref, label_ref):
    row = iota((16, DZ), 0)
    token = iota((DZ, TOK), 1) + 1

    def one(block_ref, i, q):
        x = block_ref[i, 0:TOK, :]
        table = block_ref[i, TOK:MROWS, :].astype(f32)

        def pick(k):
            return jnp.sum(jnp.where(row == 4 * k + y, table, 0.0), axis=0, keepdims=True)

        tok, high, low, label = pick(0), pick(1), pick(2), pick(3)
        label_ref[pl.ds(q, 1), :] = label
        cols = jnp.concatenate([tok, high, low, jnp.zeros((5, DZ), f32)], axis=0).T
        here = cols[:, 0:1].astype(i32) == token
        place = jnp.concatenate(
            [
                jnp.where(here, cols[:, 1:2], 0.0).astype(bf16),
                jnp.where(here, cols[:, 2:3], 0.0).astype(bf16),
            ],
            axis=1,
        )
        rows = dot(place, jnp.concatenate([x, x], axis=0)).astype(bf16)
        rows_ref[:, pl.ds(pl.multiple_of(q * PCAP, PCAP), PCAP), :] = rows.reshape(EY, PCAP, DZ)

    def over(block_ref, count, first):
        def step(i, carry):
            one(block_ref, i, first + i)
            return carry

        lax.fori_loop(0, count, step, 0)

    over(own, NZ, y * NZ)
    over(left, NZ, ((y + 3) & 3) * NZ)
    over(right, NZ, ((y + 1) & 3) * NZ)
    over(far0, NZ // 2, ((y + 2) & 3) * NZ)
    over(far1, NZ // 2, ((y + 2) & 3) * NZ + NZ // 2)


def back_kernel(y_ref, own, left, right, far0, far1, m2_ref, out_ref, label_ref, rows_ref):
    gather_rows(y_ref[0], own, left, right, far0, far1, rows_ref, label_ref)

    def owner(zo, carry):
        for j in range(EO):
            out_ref[zo, j * R : (j + 1) * R, :] = dot(
                m2_ref[zo, j * R : (j + 1) * R, :], rows_ref[zo * EO + j], 1, 1
            ).astype(bf16)
        return carry

    lax.fori_loop(0, NZ, owner, 0)


def squares(v):
    v = v * v
    total = v[:, 0:128]
    for c in range(1, v.shape[1] // 128):
        total = total + v[:, c * 128 : (c + 1) * 128]
    return total


def spread(label, value):
    label = jnp.broadcast_to(label, value.shape)
    return jnp.concatenate(
        [jnp.where(label == n + 1.0, value, 0.0).astype(bf16) for n in range(NEX)], axis=0
    )


def b_kernel(y_ref, own, left, right, far0, far1, low_ref, lab_ref, out_ref, sq_ref, rows_ref, unused_ref):
    i = pl.program_id(0)

    @pl.when(i == 0)
    def _():
        gather_rows(y_ref[0], own, left, right, far0, far1, rows_ref, unused_ref)
        sq_ref[...] = jnp.zeros_like(sq_ref)

    for j in range(EO):
        low = low_ref[i, j * R : (j + 1) * R, :].astype(f32)
        b = dot(spread(lab_ref[0, j : j + 1, :], low), rows_ref[i * EO + j])
        sq_ref[...] += squares(b)
        out_ref[j] = b.astype(bf16)


def a_kernel(back_ref, lab_ref, hidden_ref, down_ref, sqb_ref, grad_ref, a_ref, norm_ref, sq_ref):
    j = pl.program_id(0)

    @pl.when(j == 0)
    def _():
        sq_ref[...] = sqb_ref[...]

    at = pl.multiple_of(j * R, R)
    total = back_ref[0, pl.ds(at, R), :].astype(f32)
    for z in range(1, NZ):
        total = total + back_ref[z, pl.ds(at, R), :].astype(f32)
    pad = pad_matrix()
    back = dot(total.astype(bf16), pad, 1, 1)
    label = dot(jnp.broadcast_to(lab_ref[0], (16, PSLOTS)).astype(bf16), pad, 1, 1)[0:1]
    grad_ref[0] = (SCALE * dot(back.astype(bf16), down_ref[0], 0, 0)).astype(bf16)
    a = dot(spread(label, back), hidden_ref[0])
    sq_ref[...] += squares(a)
    a_ref[0] = a.astype(bf16)

    @pl.when(j == EO - 1)
    def _():
        s = jnp.sum(sq_ref[...].reshape(NEX, R, 128), axis=1)
        s = jnp.broadcast_to(jnp.sum(s, axis=1, keepdims=True), (NEX, 128)) * (SCALE * SCALE)
        s = jnp.where(iota((8, 128), 1) < 64, s[0:8], s[8:16])
        norm_ref[...] = jnp.broadcast_to(s[None], norm_ref.shape)


def clip_kernel(norm_ref, b_ref, a_ref, out_ref, ga_ref):
    i = pl.program_id(0)
    radius = math.sqrt(EXP * R * (D + F) / (DP * NEX))
    norm = norm_ref[0]
    for q in range(1, NSRC):
        norm = norm + norm_ref[q]
    other = pltpu.roll(norm, 64, 1)
    first = iota((8, 128), 1) < 64
    norm = jnp.concatenate(
        [jnp.where(first, norm, other), jnp.where(first, other, norm)], axis=0
    )
    factor = SCALE * radius / (jnp.sqrt(norm) + GAMMA)

    def weighted(ref, j, width):
        tiles = []
        for c in range(width // 128):
            total = None
            for n in range(NEX):
                term = ref[j, n * R : (n + 1) * R, c * 128 : (c + 1) * 128].astype(f32) * factor[n : n + 1]
                total = term if total is None else total + term
            tiles.append(total)
        return jnp.concatenate(tiles, axis=1)

    @pl.when(i == 0)
    def _():
        for j in range(EO):
            ga_ref[j * R : (j + 1) * R, :] = weighted(a_ref, j, F)
        for d in range(DP):
            out_ref[d, :, DZ : DZ + FA] = ga_ref[:, d * FA : (d + 1) * FA].astype(bf16)

    for j in range(EO):
        out_ref[i, j * R : (j + 1) * R, 0:DZ] = weighted(b_ref, j, DZ).astype(bf16)


def shape(*dims, dtype=bf16):
    return jax.ShapeDtypeStruct(dims, dtype)


def whole(*dims):
    return pl.BlockSpec(dims, lambda i: (0,) * len(dims))


def call(kernel, name, flops, moved, **kw):
    return pl.pallas_call(
        kernel,
        name=name,
        compiler_params=pltpu.CompilerParams(**PARAMS),
        cost_estimate=pl.CostEstimate(flops=flops, bytes_accessed=moved, transcendentals=0),
        **kw,
    )


def shards(grad, gates, routes, example, hidden, down, up):
    me = lax.axis_index("expert")
    y = (me // NZ).astype(i32)
    z = me % NZ
    hidden = hidden[0]

    m1 = call(
        send_kernel, "send", 1 << 28, 3 << 20,
        in_specs=[VMEM] * 4, out_specs=VMEM, out_shape=shape(NZ, MROWS, DZ),
    )(grad[0], gates[0], routes[0], example)
    own = lax.all_to_all(m1, "expert", 0, 0, axis_index_groups=ZGROUPS, tiled=True)

    m2 = call(
        low_kernel, "low", 1 << 28, 7 << 20,
        grid=(EO,),
        in_specs=[
            pl.BlockSpec((1, SLOTS, F), lambda i: (i, 0, 0)),
            pl.BlockSpec((1, R, F), lambda i: (i, 0, 0)),
            pl.BlockSpec((1, R, D), lambda i: (i, 0, 0)),
        ],
        out_specs=whole(NZ, 2 * EO * R, DZ),
        out_shape=shape(NZ, 2 * EO * R, DZ),
    )(hidden, down, up)
    m2r = lax.all_to_all(m2, "expert", 0, 0, axis_index_groups=ZGROUPS, tiled=True)

    def over_y(v, k):
        pairs = [(a * NZ + b, ((a + k) % NY) * NZ + b) for a in range(NY) for b in range(NZ)]
        return lax.ppermute(v, "expert", pairs)

    left = over_y(own, 1)
    right = over_y(own, NY - 1)
    far0 = over_y(left[: NZ // 2], 1)
    far1 = over_y(right[NZ // 2 :], NY - 1)
    blocks = (own, left, right, far0, far1)
    here = y.reshape(1)

    back, labels = call(
        back_kernel, "back", 3 << 30, 8 << 20,
        in_specs=[SMEM] + [VMEM] * 6,
        out_specs=[VMEM, VMEM],
        out_shape=[shape(NZ, EO * R, PSLOTS), shape(NSRC, EY * PCAP, dtype=f32)],
        scratch_shapes=[pltpu.VMEM((EY, PSLOTS, DZ), bf16)],
    )(here, *blocks, m2r)
    backr = lax.all_to_all(back, "expert", 0, 0, axis_index_groups=ZGROUPS, tiled=True)
    labels = labels.reshape(NSRC, EY, PCAP).transpose(1, 0, 2).reshape(NZ, EO, PSLOTS)
    own_labels = lax.dynamic_index_in_dim(labels, z, 0, keepdims=False).reshape(EO, 1, PSLOTS)

    big_b, sq_b = call(
        b_kernel, "norm_b", 6 << 30, 18 << 20,
        grid=(NZ,),
        in_specs=[SMEM]
        + [whole(NZ, MROWS, DZ)] * 3
        + [whole(NZ // 2, MROWS, DZ)] * 2
        + [
            whole(NZ, EO * R, PSLOTS),
            pl.BlockSpec((1, EO, PSLOTS), lambda i: (i, 0, 0)),
        ],
        out_specs=[
            pl.BlockSpec((EO, NEX * R, DZ), lambda i: (i, 0, 0)),
            whole(NEX * R, 128),
        ],
        out_shape=[shape(EY, NEX * R, DZ), shape(NEX * R, 128, dtype=f32)],
        scratch_shapes=[
            pltpu.VMEM((EY, PSLOTS, DZ), bf16),
            pltpu.VMEM((NSRC, EY * PCAP), f32),
        ],
    )(here, *blocks, m2r[:, EO * R :], labels)

    hidden_grad, big_a, norm = call(
        a_kernel, "norm_a", 2 << 30, 14 << 20,
        grid=(EO,),
        in_specs=[
            whole(NZ, EO * R, PSLOTS),
            pl.BlockSpec((1, 1, PSLOTS), lambda i: (i, 0, 0)),
            pl.BlockSpec((1, SLOTS, F), lambda i: (i, 0, 0)),
            pl.BlockSpec((1, R, F), lambda i: (i, 0, 0)),
            whole(NEX * R, 128),
        ],
        out_specs=[
            pl.BlockSpec((1, SLOTS, F), lambda i: (i, 0, 0)),
            pl.BlockSpec((1, NEX * R, F), lambda i: (i, 0, 0)),
            whole(NSRC, 8, 128),
        ],
        out_shape=[
            shape(EO, SLOTS, F),
            shape(EO, NEX * R, F),
            shape(NSRC, 8, 128, dtype=f32),
        ],
        scratch_shapes=[pltpu.VMEM((NEX * R, 128), f32)],
    )(backr, own_labels, hidden, down, sq_b)
    norm = lax.all_to_all(norm, "expert", 0, 0, tiled=True)

    sums = call(
        clip_kernel, "clip", 1 << 20, 12 << 20,
        grid=(NZ,),
        in_specs=[
            whole(NSRC, 8, 128),
            pl.BlockSpec((EO, NEX * R, DZ), lambda i: (i, 0, 0)),
            whole(EO, NEX * R, F),
        ],
        out_specs=whole(DP, EO * R, DZ + FA),
        out_shape=shape(DP, EO * R, DZ + FA),
        scratch_shapes=[pltpu.VMEM((EO * R, F), f32)],
    )(norm, big_b, big_a)
    sums = jnp.sum(lax.all_to_all(sums, "dp", 0, 0, tiled=True).astype(f32), axis=0)
    swap = [
        ((g * NY + a) * NZ + b, (b * NY + a) * NZ + g)
        for g in range(DP) for a in range(NY) for b in range(NZ)
    ]
    grad_b = lax.ppermute(sums[:, :DZ], ("dp", "expert"), swap)
    return (
        hidden_grad[None],
        sums[:, DZ:].reshape(EO, R, FA),
        grad_b.reshape(EO, R, DZ),
    )


def solution(mesh):
    return jax.shard_map(
        shards,
        mesh=mesh,
        in_specs=(
            P("dp", "expert", None),
            P("dp", "expert", None),
            P("dp", "expert", None),
            P("dp", "expert"),
            P("dp", "expert", None, None),
            P("expert", None, None),
            P("expert", None, None),
        ),
        out_specs=(P("dp", "expert", None, None), P("expert", None, "dp"), P("expert", None, "dp")),
        check_vma=False,
    )
```

```python
import math

import jax
import jax.numpy as jnp
from jax import lax
from jax.experimental import pallas as pl
from jax.experimental.pallas import tpu as pltpu
from jax.sharding import PartitionSpec as P

NY, NZ, DP = 4, 8, 8
NSRC = NY * NZ
TOK = 128
TOPK = 8
D = 4096
DZ = D // NZ
F = 1536
R = 16
EXP = 128
EO = 4
EY = EXP // NY
CAP = 12
PCAP = 16
SLOTS = NSRC * CAP
PSLOTS = NSRC * PCAP
NEX = 16
MROWS = TOK + 16
SCALE = 2.0
GAMMA = 0.01
FA = F // DP
f32 = jnp.float32
bf16 = jnp.bfloat16
i32 = jnp.int32

ZGROUPS = [[y * NZ + z for z in range(NZ)] for y in range(NY)]
XYGROUPS = [
    [g * NSRC + y * NZ + z for g in range(DP) for y in range(NY)] for z in range(NZ)
]
VMEM = pl.BlockSpec(memory_space=pltpu.VMEM)
SMEM = pl.BlockSpec(memory_space=pltpu.SMEM)
PARAMS = dict(vmem_limit_bytes=56 * 1024 * 1024)


def dot(a, b, ca=1, cb=0):
    return lax.dot_general(a, b, (((ca,), (cb,)), ((), ())), preferred_element_type=f32)


def iota(shape, dim):
    return lax.broadcasted_iota(i32, shape, dim)


def pad_matrix():
    lane = iota((SLOTS, PSLOTS), 1)
    s = lane & (PCAP - 1)
    at = (lane >> 4) * CAP + s
    return jnp.where((at == iota((SLOTS, PSLOTS), 0)) & (s < CAP), 1.0, 0.0).astype(bf16)


def send_kernel(x_ref, gate_ref, route_ref, example_ref, out_ref):
    gate_of = gate_ref[...].T
    route_of = route_ref[...].astype(f32).T.astype(i32)
    expert = iota((TOK, EXP), 1)
    routed = jnp.zeros((TOK, EXP), f32)
    gate = jnp.zeros((TOK, EXP), f32)
    for k in range(TOPK):
        hit = route_of[:, k : k + 1] == expert
        routed = jnp.where(hit, 1.0, routed)
        gate = jnp.where(hit, gate_of[:, k : k + 1], gate)
    before = jnp.where(iota((TOK, TOK), 1) < iota((TOK, TOK), 0), 1.0, 0.0).astype(bf16)
    rank = jnp.where(routed > 0.5, dot(before, routed.astype(bf16)), 64.0).astype(bf16)
    high = gate.astype(bf16)
    low = (gate - high.astype(f32)).astype(bf16)
    row = iota((16, TOK), 0)
    ids = jnp.where(
        row == 0,
        iota((16, TOK), 1) + 1,
        jnp.where(row == 1, jnp.broadcast_to(example_ref[...], (16, TOK)) + 1, 0),
    ).astype(f32).astype(bf16)
    ones = jnp.ones((16, TOK), bf16)
    toks, highs, lows, labels = [], [], [], []
    for y in range(NY):
        lane = iota((EXP, EY * PCAP), 1)
        expand = jnp.where((lane >> 4) + y * EY == iota((EXP, EY * PCAP), 0), 1.0, 0.0).astype(bf16)
        place = (iota((TOK, EY * PCAP), 1) & (PCAP - 1)).astype(f32)
        here = dot(rank, expand) == place
        tab = dot(ids, jnp.where(here, 1.0, 0.0).astype(bf16))
        toks.append(tab[0:1])
        labels.append(tab[1:2])
        highs.append(dot(ones, jnp.where(here, dot(high, expand), 0.0).astype(bf16))[0:1])
        lows.append(dot(ones, jnp.where(here, dot(low, expand), 0.0).astype(bf16))[0:1])
    table = jnp.concatenate(toks + highs + lows + labels, axis=0).astype(bf16)
    for z in range(NZ):
        out_ref[z, 0:TOK, :] = x_ref[:, z * DZ : (z + 1) * DZ]
        out_ref[z, TOK:MROWS, :] = table


def low_kernel(hidden_ref, down_ref, out_ref):
    j = pl.program_id(0)
    low = dot(down_ref[0], hidden_ref[0], 1, 1).astype(bf16)
    low = dot(low, pad_matrix()).astype(bf16)
    at = pl.multiple_of(j * R, R)
    for z in range(NZ):
        out_ref[z, pl.ds(at, R), :] = low


def gather_kernel(y_ref, *refs):
    blocks, (rows_ref, label_ref) = refs[:-2], refs[-2:]
    y = y_ref[0]
    row = iota((16, DZ), 0)
    token = iota((DZ, TOK), 1) + 1
    q = 0
    for block_ref in blocks:
        for i in range(block_ref.shape[0]):
            x = block_ref[i, 0:TOK, :]
            table = block_ref[i, TOK:MROWS, :].astype(f32)

            def pick(k):
                return jnp.sum(jnp.where(row == 4 * k + y, table, 0.0), axis=0, keepdims=True)

            tok, high, low, label = pick(0), pick(1), pick(2), pick(3)
            label_ref[q : q + 1, :] = label
            cols = jnp.concatenate([tok, high, low, jnp.zeros((5, DZ), f32)], axis=0).T
            here = cols[:, 0:1].astype(i32) == token
            place = jnp.concatenate(
                [
                    jnp.where(here, cols[:, 1:2], 0.0).astype(bf16),
                    jnp.where(here, cols[:, 2:3], 0.0).astype(bf16),
                ],
                axis=1,
            )
            rows = dot(place, jnp.concatenate([x, x], axis=0)).astype(bf16)
            rows_ref[:, q * PCAP : (q + 1) * PCAP, :] = rows.reshape(EY, PCAP, DZ)
            q += 1


def back_kernel(own_ref, up_ref, out_ref):
    token = (iota((TOK, 256), 0) + 1).astype(f32)
    group = iota((R, 256), 1) >> 4
    first = iota((R, 128), 1) < 64

    def pair(p, carry):
        x = jnp.concatenate([own_ref[2 * p, 0:TOK, :], own_ref[2 * p + 1, 0:TOK, :]], axis=0)
        tables = [own_ref[2 * p + h, TOK:MROWS, :].astype(f32) for h in range(2)]
        at = pl.multiple_of(p * R, R)
        for y in range(NY):
            up = jnp.concatenate([up_ref[g * NY + y] for g in range(DP)], axis=0)
            dense = dot(up, x, 1, 1)
            dense = jnp.concatenate(
                [dense[g * 64 + zo * 8 : g * 64 + zo * 8 + 8] for zo in range(NZ) for g in range(DP)],
                axis=0,
            )
            high = dense.astype(bf16)
            low = (dense - high.astype(f32)).astype(bf16)
            for c in range(2):
                found = []
                for h in range(2):
                    def entry(k):
                        return tables[h][4 * k + y : 4 * k + y + 1, c * 256 : (c + 1) * 256]

                    place = jnp.where(entry(0) == token, 1.0, 0.0).astype(bf16)
                    part = dot(
                        jnp.concatenate(
                            [
                                v[c * 256 : (c + 1) * 256, h * TOK : (h + 1) * TOK]
                                for v in (high, low)
                            ],
                            axis=1,
                        ),
                        jnp.concatenate([place, place], axis=0),
                    )
                    total = jnp.where(group == 0, part[0:R], 0.0)
                    for e in range(1, 16):
                        total = jnp.where(group == e, part[e * R : (e + 1) * R], total)
                    found.append(total * (entry(1) + entry(2)))
                for t in range(2):
                    a, b = (v[:, t * 128 : (t + 1) * 128] for v in found)
                    o = y * NZ + c * 4 + t * 2
                    out_ref[o, pl.ds(at, R), :] = jnp.where(first, a, pltpu.roll(b, 64, 1)).astype(bf16)
                    out_ref[o + 1, pl.ds(at, R), :] = jnp.where(first, pltpu.roll(a, 64, 1), b).astype(bf16)
        return carry

    lax.fori_loop(0, NZ // 2, pair, 0)


def squares(v):
    v = v * v
    total = v[:, 0:128]
    for c in range(1, v.shape[1] // 128):
        total = total + v[:, c * 128 : (c + 1) * 128]
    return total


def spread(label, value):
    label = jnp.broadcast_to(label, value.shape)
    return jnp.concatenate(
        [jnp.where(label == n + 1.0, value, 0.0).astype(bf16) for n in range(NEX)], axis=0
    )


def absolute(y, k):
    return pl.multiple_of(((k - y) & 3) * (NZ * PCAP), NZ * PCAP)


def b_kernel(y_ref, own, right, far, left, low_ref, lab_ref, out_ref, sq_ref):
    i = pl.program_id(0)
    y = y_ref[0]

    @pl.when(i == 0)
    def _():
        sq_ref[...] = jnp.zeros_like(sq_ref)

    for j in range(EO):
        low = jnp.concatenate(
            [
                low_ref[i, j * R : (j + 1) * R, pl.ds(pl.multiple_of(((y + k) & 3) * 128, 128), 128)]
                for k in range(NY)
            ],
            axis=1,
        ).astype(f32)
        rows = jnp.concatenate([own[j], right[j], far[j], left[j]], axis=0)
        b = dot(spread(lab_ref[0, j : j + 1, :], low), rows)
        sq_ref[...] += squares(b)
        out_ref[j] = b.astype(bf16)


def a_kernel(y_ref, back_ref, lab_ref, hidden_ref, down_ref, sqb_ref, grad_ref, a_ref, norm_ref, sq_ref, total_ref):
    j = pl.program_id(0)
    y = y_ref[0]

    @pl.when(j == 0)
    def _():
        sq_ref[...] = sqb_ref[...]
        for k in range(NY):
            total = back_ref[k * NZ].astype(f32)
            for z in range(1, NZ):
                total = total + back_ref[k * NZ + z].astype(f32)
            for p in range(NZ // 2):
                at = (k * 4 + p) * 128
                total_ref[:, at : at + 128] = total[p * R : (p + 1) * R].astype(bf16)

    tiles = []
    for c in range(3):
        lane = iota((768, 128), 0) + c * 640
        s = lane & (PCAP - 1)
        at = jnp.where(((lane >> 4) & 3 == j) & (s < CAP), (lane >> 6) * CAP + s, -1)
        pick = jnp.where(at == iota((768, 128), 1) + c * 128, 1.0, 0.0).astype(bf16)
        tiles.append(dot(total_ref[:, c * 640 : c * 640 + 768], pick))
    back = jnp.concatenate(tiles, axis=1)
    label = jnp.concatenate([lab_ref[0, :, pl.ds(absolute(y, k), 128)] for k in range(NY)], axis=1)
    label = dot(jnp.broadcast_to(label, (16, PSLOTS)).astype(bf16), pad_matrix(), 1, 1)[0:1]
    grad_ref[0] = (SCALE * dot(back.astype(bf16), down_ref[0], 0, 0)).astype(bf16)
    a = dot(spread(label, back), hidden_ref[0])
    sq_ref[...] += squares(a)
    a_ref[0] = a.astype(bf16)

    @pl.when(j == EO - 1)
    def _():
        s = jnp.sum(sq_ref[...].reshape(NEX, R, 128), axis=1)
        s = jnp.broadcast_to(jnp.sum(s, axis=1, keepdims=True), (NEX, 128)) * (SCALE * SCALE)
        s = jnp.where(iota((8, 128), 1) < 64, s[0:8], s[8:16])
        norm_ref[...] = jnp.broadcast_to(s[None], norm_ref.shape)


def clip_kernel(norm_ref, b_ref, a_ref, out_ref, ga_ref):
    i = pl.program_id(0)
    radius = math.sqrt(EXP * R * (D + F) / (DP * NEX))
    norm = norm_ref[0]
    for q in range(1, NSRC):
        norm = norm + norm_ref[q]
    other = pltpu.roll(norm, 64, 1)
    first = iota((8, 128), 1) < 64
    norm = jnp.concatenate(
        [jnp.where(first, norm, other), jnp.where(first, other, norm)], axis=0
    )
    factor = SCALE * radius / (jnp.sqrt(norm) + GAMMA)

    def weighted(ref, j, width):
        tiles = []
        for c in range(width // 128):
            total = None
            for n in range(NEX):
                term = ref[j, n * R : (n + 1) * R, c * 128 : (c + 1) * 128].astype(f32) * factor[n : n + 1]
                total = term if total is None else total + term
            tiles.append(total)
        return jnp.concatenate(tiles, axis=1)

    @pl.when(i == 0)
    def _():
        for j in range(EO):
            ga_ref[j * R : (j + 1) * R, :] = weighted(a_ref, j, F)
        for d in range(DP):
            out_ref[d, :, DZ : DZ + FA] = ga_ref[:, d * FA : (d + 1) * FA].astype(bf16)

    for j in range(EO):
        out_ref[i, j * R : (j + 1) * R, 0:DZ] = weighted(b_ref, j, DZ).astype(bf16)


def shape(*dims, dtype=bf16):
    return jax.ShapeDtypeStruct(dims, dtype)


def whole(*dims):
    return pl.BlockSpec(dims, lambda i: (0,) * len(dims))


def call(kernel, name, flops, moved, **kw):
    return pl.pallas_call(
        kernel,
        name=name,
        compiler_params=pltpu.CompilerParams(**PARAMS),
        cost_estimate=pl.CostEstimate(flops=flops, bytes_accessed=moved, transcendentals=0),
        **kw,
    )


def shards(grad, gates, routes, example, hidden, down, up):
    me = lax.axis_index("expert")
    y = (me // NZ).astype(i32)
    z = me % NZ
    here = y.reshape(1)
    hidden = hidden[0]

    part = lax.dynamic_slice_in_dim(up.reshape(EO * R, D), lax.axis_index("dp") * 8, 8, 0)
    part = part.reshape(8, NZ, DZ).transpose(1, 0, 2)
    part = lax.all_to_all(part, "expert", 0, 0, axis_index_groups=ZGROUPS, tiled=True)
    part = jnp.broadcast_to(part.reshape(1, NZ * 8, DZ), (DP * NY, NZ * 8, DZ))
    ups = lax.all_to_all(part, ("dp", "expert"), 0, 0, axis_index_groups=XYGROUPS, tiled=True)

    m1 = call(
        send_kernel, "send", 2 << 30, 3 << 20,
        in_specs=[VMEM] * 4, out_specs=VMEM, out_shape=shape(NZ, MROWS, DZ),
    )(grad[0], gates[0].T, routes[0].T, example)
    own = lax.all_to_all(m1, "expert", 0, 0, axis_index_groups=ZGROUPS, tiled=True)

    def over_y(v, k):
        pairs = [(a * NZ + b, ((a + k) % NY) * NZ + b) for a in range(NY) for b in range(NZ)]
        return lax.ppermute(v, "expert", pairs)

    left = over_y(own, 1)
    right = over_y(own, NY - 1)
    far0 = over_y(left[: NZ // 2], 1)
    far1 = over_y(right[NZ // 2 :], NY - 1)

    low = call(
        low_kernel, "low", 2 << 30, 7 << 20,
        grid=(EO,),
        in_specs=[
            pl.BlockSpec((1, SLOTS, F), lambda i: (i, 0, 0)),
            pl.BlockSpec((1, R, F), lambda i: (i, 0, 0)),
        ],
        out_specs=whole(NZ, EO * R, DZ),
        out_shape=shape(NZ, EO * R, DZ),
    )(hidden, down)
    low = lax.all_to_all(low, "expert", 0, 0, axis_index_groups=ZGROUPS, tiled=True)

    def gather(*blocks):
        return call(
            gather_kernel, "gather", 4 << 30, 8 << 20,
            in_specs=[SMEM] + [VMEM] * len(blocks),
            out_specs=[VMEM, VMEM],
            out_shape=[shape(EY, NZ * PCAP, DZ), shape(NZ, EY * PCAP, dtype=f32)],
        )(here, *blocks)

    back = call(
        back_kernel, "back", 6 << 30, 6 << 20,
        in_specs=[VMEM] * 2, out_specs=VMEM, out_shape=shape(NSRC, EO * R, 128),
    )(own, ups)
    back = lax.all_to_all(back, "expert", 0, 0, tiled=True)

    parts = [gather(own), gather(right), gather(far0, far1), gather(left)]
    rows = [v[0] for v in parts]
    labels = jnp.stack([v[1] for v in parts]).reshape(NY * NZ, EY, PCAP)
    labels = labels.transpose(1, 0, 2).reshape(NZ, EO, PSLOTS)
    own_labels = lax.dynamic_index_in_dim(labels, z, 0, keepdims=False).reshape(EO, 1, PSLOTS)

    big_b, sq_b = call(
        b_kernel, "norm_b", 6 << 30, 26 << 20,
        grid=(NZ,),
        in_specs=[SMEM]
        + [pl.BlockSpec((EO, NZ * PCAP, DZ), lambda i: (i, 0, 0))] * 4
        + [
            whole(NZ, EO * R, PSLOTS),
            pl.BlockSpec((1, EO, PSLOTS), lambda i: (i, 0, 0)),
        ],
        out_specs=[
            pl.BlockSpec((EO, NEX * R, DZ), lambda i: (i, 0, 0)),
            whole(NEX * R, 128),
        ],
        out_shape=[shape(EY, NEX * R, DZ), shape(NEX * R, 128, dtype=f32)],
    )(here, *rows, low, labels)

    hidden_grad, big_a, norm = call(
        a_kernel, "norm_a", 6 << 30, 14 << 20,
        grid=(EO,),
        in_specs=[
            SMEM,
            whole(NSRC, EO * R, 128),
            pl.BlockSpec((1, 1, PSLOTS), lambda i: (i, 0, 0)),
            pl.BlockSpec((1, SLOTS, F), lambda i: (i, 0, 0)),
            pl.BlockSpec((1, R, F), lambda i: (i, 0, 0)),
            whole(NEX * R, 128),
        ],
        out_specs=[
            pl.BlockSpec((1, SLOTS, F), lambda i: (i, 0, 0)),
            pl.BlockSpec((1, NEX * R, F), lambda i: (i, 0, 0)),
            whole(NSRC, 8, 128),
        ],
        out_shape=[
            shape(EO, SLOTS, F),
            shape(EO, NEX * R, F),
            shape(NSRC, 8, 128, dtype=f32),
        ],
        scratch_shapes=[pltpu.VMEM((NEX * R, 128), f32), pltpu.VMEM((R, NSRC * 64), bf16)],
    )(here, back, own_labels, hidden, down, sq_b)
    norm = lax.all_to_all(norm, "expert", 0, 0, tiled=True)

    sums = call(
        clip_kernel, "clip", 1 << 20, 12 << 20,
        grid=(NZ,),
        in_specs=[
            whole(NSRC, 8, 128),
            pl.BlockSpec((EO, NEX * R, DZ), lambda i: (i, 0, 0)),
            whole(EO, NEX * R, F),
        ],
        out_specs=whole(DP, EO * R, DZ + FA),
        out_shape=shape(DP, EO * R, DZ + FA),
        scratch_shapes=[pltpu.VMEM((EO * R, F), f32)],
    )(norm, big_b, big_a)
    sums = jnp.sum(lax.all_to_all(sums, "dp", 0, 0, tiled=True).astype(f32), axis=0)
    swap = [
        ((g * NY + a) * NZ + b, (b * NY + a) * NZ + g)
        for g in range(DP) for a in range(NY) for b in range(NZ)
    ]
    grad_b = lax.ppermute(sums[:, :DZ], ("dp", "expert"), swap)
    return (
        hidden_grad[None],
        sums[:, DZ:].reshape(EO, R, FA),
        grad_b.reshape(EO, R, DZ),
    )


def solution(mesh):
    return jax.shard_map(
        shards,
        mesh=mesh,
        in_specs=(
            P("dp", "expert", None),
            P("dp", "expert", None),
            P("dp", "expert", None),
            P("dp", "expert"),
            P("dp", "expert", None, None),
            P("expert", None, None),
            P("expert", None, None),
        ),
        out_specs=(P("dp", "expert", None, None), P("expert", None, "dp"), P("expert", None, "dp")),
        check_vma=False,
    )
```

```python
import math

import jax
import jax.numpy as jnp
from jax import lax
from jax.experimental import pallas as pl
from jax.experimental.pallas import tpu as pltpu
from jax.sharding import PartitionSpec as P

NY, NZ, DP = 4, 8, 8
NSRC = NY * NZ
TOK = 128
TOPK = 8
D = 4096
DZ = D // NZ
F = 1536
R = 16
EXP = 128
EO = 4
EY = EXP // NY
CAP = 12
PCAP = 16
SLOTS = NSRC * CAP
PSLOTS = NSRC * PCAP
NEX = 16
MROWS = TOK + 16
SCALE = 2.0
GAMMA = 0.01
FA = F // DP
f32 = jnp.float32
bf16 = jnp.bfloat16
i32 = jnp.int32

ZGROUPS = [[y * NZ + z for z in range(NZ)] for y in range(NY)]
RING = (0, 3, 1, 2)
LOWS = ((0, -1, 1), (-3, -4, -2), (3, 2))
HALF = EY * PCAP // 2
BROWS = EO * R + 16
VMEM = pl.BlockSpec(memory_space=pltpu.VMEM)
SMEM = pl.BlockSpec(memory_space=pltpu.SMEM)
PARAMS = dict(vmem_limit_bytes=14 * 1024 * 1024)


def dot(a, b, ca=1, cb=0):
    return lax.dot_general(a, b, (((ca,), (cb,)), ((), ())), preferred_element_type=f32)


def iota(shape, dim):
    return lax.broadcasted_iota(i32, shape, dim)


def pad_matrix():
    lane = iota((SLOTS, PSLOTS), 1)
    s = lane & (PCAP - 1)
    at = (lane >> 4) * CAP + s
    return jnp.where((at == iota((SLOTS, PSLOTS), 0)) & (s < CAP), 1.0, 0.0).astype(bf16)


def send_kernel(x_ref, gate_ref, route_ref, example_ref, out_ref):
    gate_of = gate_ref[...].T
    route_of = route_ref[...].astype(f32).T.astype(i32)
    expert = iota((TOK, EXP), 1)
    routed = jnp.zeros((TOK, EXP), f32)
    gate = jnp.zeros((TOK, EXP), f32)
    for k in range(TOPK):
        hit = route_of[:, k : k + 1] == expert
        routed = jnp.where(hit, 1.0, routed)
        gate = jnp.where(hit, gate_of[:, k : k + 1], gate)
    before = jnp.where(iota((TOK, TOK), 1) < iota((TOK, TOK), 0), 1.0, 0.0).astype(bf16)
    rank = jnp.where(routed > 0.5, dot(before, routed.astype(bf16)), 64.0).astype(bf16)
    high = gate.astype(bf16)
    low = (gate - high.astype(f32)).astype(bf16)
    row = iota((16, TOK), 0)
    ids = jnp.where(
        row == 0,
        iota((16, TOK), 1) + 1,
        jnp.where(row == 1, jnp.broadcast_to(example_ref[...], (16, TOK)) + 1, 0),
    ).astype(f32).astype(bf16)
    ones = jnp.ones((16, TOK), bf16)
    toks, highs, lows, labels = [], [], [], []
    for y in range(NY):
        lane = iota((EXP, EY * PCAP), 1)
        expand = jnp.where((lane >> 4) + y * EY == iota((EXP, EY * PCAP), 0), 1.0, 0.0).astype(bf16)
        place = (iota((TOK, EY * PCAP), 1) & (PCAP - 1)).astype(f32)
        here = dot(rank, expand) == place
        tab = dot(ids, jnp.where(here, 1.0, 0.0).astype(bf16))
        toks.append(tab[0:1])
        labels.append(tab[1:2])
        highs.append(dot(ones, jnp.where(here, dot(high, expand), 0.0).astype(bf16))[0:1])
        lows.append(dot(ones, jnp.where(here, dot(low, expand), 0.0).astype(bf16))[0:1])
    table = jnp.concatenate(toks + highs + lows + labels, axis=0).astype(bf16)
    for z in range(NZ):
        out_ref[z, 0:TOK, :] = x_ref[:, z * DZ : (z + 1) * DZ]
        out_ref[z, TOK:MROWS, :] = table


def low_kernel(hidden_ref, down_ref, out_ref):
    low = dot(down_ref[0], hidden_ref[0], 1, 1).astype(bf16)
    low = dot(low, pad_matrix()).astype(bf16)
    out_ref[...] = low


def gather_kernel(y_ref, *refs):
    blocks, (rows_ref, label_ref) = refs[:-2], refs[-2:]
    y = y_ref[0]
    lanes = pl.ds(pl.multiple_of(pl.program_id(0) * HALF, HALF), HALF)
    row = iota((16, HALF), 0)
    token = iota((HALF, TOK), 1) + 1
    lane = iota((EY // 2, HALF), 1)
    expert = iota((EY // 2, HALF), 0)
    labels = jnp.zeros((EY // 2, NZ * PCAP), f32)
    q = 0
    for block_ref in blocks:
        for i in range(block_ref.shape[0]):
            x = block_ref[i, 0:TOK, :]
            table = block_ref[i, TOK:MROWS, lanes].astype(f32)

            def pick(k):
                return jnp.sum(jnp.where(row == 4 * k + y, table, 0.0), axis=0, keepdims=True)

            tok, high, low, label = pick(0), pick(1), pick(2), pick(3)
            here = jnp.where(lane >> 4 == expert, label, 0.0).astype(bf16)
            at = (iota((HALF, NZ * PCAP), 0) & (PCAP - 1)) + q * PCAP
            move = jnp.where(at == iota((HALF, NZ * PCAP), 1), 1.0, 0.0).astype(bf16)
            labels = labels + dot(here, move)
            cols = jnp.concatenate([tok, high, low, jnp.zeros((5, HALF), f32)], axis=0).T
            here = cols[:, 0:1].astype(i32) == token
            place = jnp.concatenate(
                [
                    jnp.where(here, cols[:, 1:2], 0.0).astype(bf16),
                    jnp.where(here, cols[:, 2:3], 0.0).astype(bf16),
                ],
                axis=1,
            )
            rows = dot(place, jnp.concatenate([x, x], axis=0)).astype(bf16)
            rows_ref[:, q * PCAP : (q + 1) * PCAP, :] = rows.reshape(EY // 2, PCAP, DZ)
            q += 1
    for i in range(NZ // 2):
        label_ref[i] = labels[i * EO : (i + 1) * EO]


def back_kernel(at_ref, own_ref, mine_ref, other_ref, out_ref, up_ref, table_ref):
    me_y, me_x, me_core = at_ref[0], at_ref[1], at_ref[2]
    token = (iota((TOK, 256), 0) + 1).astype(f32)
    group = iota((R, 256), 1) >> 4
    first = iota((R, 128), 1) < 64
    for k in range(NY):
        g = ((me_x + RING[k]) & 3) * 2
        up_ref[g + me_core] = mine_ref[k]
        up_ref[g + 1 - me_core] = other_ref[k]
    for q in range(NZ):
        table_ref[q] = own_ref[q, TOK:MROWS, :].astype(f32)

    def pair(p, carry):
        x = jnp.concatenate([own_ref[2 * p, 0:TOK, :], own_ref[2 * p + 1, 0:TOK, :]], axis=0)
        at = pl.multiple_of(p * R, R)
        for k in range(NY):
            y = (me_y + RING[k]) & 3
            up = jnp.concatenate([up_ref[g, k] for g in range(DP)], axis=0)
            dense = dot(up, x, 1, 1)
            dense = jnp.concatenate(
                [dense[g * 64 + zo * 8 : g * 64 + zo * 8 + 8] for zo in range(NZ) for g in range(DP)],
                axis=0,
            )
            high = dense.astype(bf16)
            low = (dense - high.astype(f32)).astype(bf16)
            for c in range(2):
                found = []
                for h in range(2):
                    def entry(kind):
                        return table_ref[2 * p + h, pl.ds(4 * kind + y, 1), c * 256 : (c + 1) * 256]

                    place = jnp.where(entry(0) == token, 1.0, 0.0).astype(bf16)
                    part = dot(
                        jnp.concatenate(
                            [
                                v[c * 256 : (c + 1) * 256, h * TOK : (h + 1) * TOK]
                                for v in (high, low)
                            ],
                            axis=1,
                        ),
                        jnp.concatenate([place, place], axis=0),
                    )
                    total = jnp.where(group == 0, part[0:R], 0.0)
                    for e in range(1, 16):
                        total = jnp.where(group == e, part[e * R : (e + 1) * R], total)
                    found.append(total * (entry(1) + entry(2)))
                for t in range(2):
                    a, b = (v[:, t * 128 : (t + 1) * 128] for v in found)
                    o = y * NZ + c * 4 + t * 2
                    out_ref[o, pl.ds(at, R), :] = jnp.where(first, a, pltpu.roll(b, 64, 1)).astype(bf16)
                    out_ref[o + 1, pl.ds(at, R), :] = jnp.where(first, pltpu.roll(a, 64, 1), b).astype(bf16)
        return carry

    lax.fori_loop(0, NZ // 2, pair, 0)

    half = iota((NZ, 128), 1) < 64
    pad = jnp.zeros((8, 128), f32)
    for y in range(NY):
        def label(h):
            rows = [table_ref[2 * p + h, 12 + y : 13 + y, :] for p in range(NZ // 2)]
            return jnp.concatenate(rows + [jnp.zeros((4, DZ), f32)], axis=0)

        even, odd = label(0), label(1)
        for t in range(4):
            a, b = even[:, t * 128 : (t + 1) * 128], odd[:, t * 128 : (t + 1) * 128]
            o = y * NZ + t * 2
            for i, v in enumerate(
                (jnp.where(half, a, pltpu.roll(b, 64, 1)), jnp.where(half, pltpu.roll(a, 64, 1), b))
            ):
                out_ref[o + i, EO * R : EO * R + 16, :] = jnp.concatenate([v, pad], axis=0).astype(bf16)


def squares(v):
    v = v * v
    total = v[:, 0:128]
    for c in range(1, v.shape[1] // 128):
        total = total + v[:, c * 128 : (c + 1) * 128]
    return total


def spread(label, value):
    label = jnp.broadcast_to(label, value.shape).astype(bf16)
    value = value.astype(bf16)
    return jnp.concatenate(
        [jnp.where(label == n + 1.0, value, jnp.zeros_like(value)) for n in range(NEX)], axis=0
    )


def b_kernel(y_ref, own, right, far, left, lab0, lab1, lab2, lab3, *refs):
    low_refs, (sqa_ref, out_ref, norm_ref, sq_ref, low_ref) = refs[:3], refs[3:]
    i = pl.program_id(0)
    y = y_ref[0]

    @pl.when(i == 0)
    def _():
        sq_ref[...] = sqa_ref[...]
        for ref, places in zip(low_refs, LOWS):
            for n, k in enumerate(places):
                low_ref[(y_ref[3] + k) & (NZ - 1)] = ref[n * EO * R : (n + 1) * EO * R, :]

    total = jnp.zeros((NEX * R, 128), f32)
    for j in range(EO):
        label = jnp.concatenate([v[0, j : j + 1, :] for v in (lab0, lab1, lab2, lab3)], axis=1)
        low = jnp.concatenate(
            [
                low_ref[i, j * R : (j + 1) * R, pl.ds(pl.multiple_of(((y + k) & 3) * 128, 128), 128)]
                for k in range(NY)
            ],
            axis=1,
        )
        rows = jnp.concatenate([own[j], right[j], far[j], left[j]], axis=0)
        b = dot(spread(label, low), rows)
        total = total + squares(b)
        out_ref[j] = b.astype(bf16)
    sq_ref[...] += total

    @pl.when(i == NZ - 1)
    def _():
        s = jnp.sum(sq_ref[...].reshape(NEX, R, 128), axis=1)
        s = jnp.broadcast_to(jnp.sum(s, axis=1, keepdims=True), (NEX, 128)) * (SCALE * SCALE)
        s = jnp.where(iota((8, 128), 1) < 64, s[0:8], s[8:16])
        norm_ref[...] = jnp.broadcast_to(s[None], norm_ref.shape)


def a_kernel(back_ref, hidden_ref, slots_ref, a_ref, sq_ref, total_ref):
    j = pl.program_id(0)

    @pl.when(j == 0)
    def _():
        sq_ref[...] = jnp.zeros_like(sq_ref)
        for k in range(NY):
            total = back_ref[k * NZ, 0 : EO * R, :].astype(f32)
            for z in range(1, NZ):
                total = total + back_ref[k * NZ + z, 0 : EO * R, :].astype(f32)
            labels = back_ref[k * NZ, EO * R : BROWS, :].astype(f32)
            for p in range(NZ // 2):
                at = (k * 4 + p) * 128
                total_ref[0:R, at : at + 128] = total[p * R : (p + 1) * R].astype(bf16)
                total_ref[R : 2 * R, at : at + 128] = jnp.broadcast_to(
                    labels[p : p + 1], (R, 128)
                ).astype(bf16)

    tiles = []
    for c in range(3):
        lane = iota((768, 128), 0) + c * 640
        s = lane & (PCAP - 1)
        at = jnp.where(((lane >> 4) & 3 == j) & (s < CAP), (lane >> 6) * CAP + s, -1)
        pick = jnp.where(at == iota((768, 128), 1) + c * 128, 1.0, 0.0).astype(bf16)
        tiles.append(dot(total_ref[:, c * 640 : c * 640 + 768], pick))
    tiles = jnp.concatenate(tiles, axis=1)
    back, label = tiles[0:R], tiles[R : R + 1]
    a = dot(spread(label, back), hidden_ref[0])
    sq_ref[...] += squares(a)
    a_ref[0] = a.astype(bf16)
    slots_ref[0] = back.astype(bf16)


def hidden_kernel(slots_ref, down_ref, grad_ref):
    grad_ref[0] = (SCALE * dot(slots_ref[0], down_ref[0], 0, 0)).astype(bf16)


def clip_kernel(norm_ref, b_ref, a_ref, out_ref, ga_ref):
    i = pl.program_id(0)
    radius = math.sqrt(EXP * R * (D + F) / (DP * NEX))
    norm = norm_ref[0]
    for q in range(1, NSRC):
        norm = norm + norm_ref[q]
    other = pltpu.roll(norm, 64, 1)
    first = iota((8, 128), 1) < 64
    norm = jnp.concatenate(
        [jnp.where(first, norm, other), jnp.where(first, other, norm)], axis=0
    )
    factor = SCALE * radius / (jnp.sqrt(norm) + GAMMA)
    wide = jnp.concatenate([factor, factor], axis=1)
    column = iota((NEX, NEX * R), 1)
    wide = jnp.sum(jnp.where(column >> 4 == iota((NEX, NEX * R), 0), wide, 0.0), axis=0, keepdims=True)
    wide = jnp.where(column & 15 == iota((R, NEX * R), 0), wide, 0.0)
    high = wide.astype(bf16)
    pick = jnp.concatenate([high, (wide - high.astype(f32)).astype(bf16)], axis=0)

    def weighted(v):
        v = dot(pick, v)
        return v[0:R] + v[R:]

    @pl.when(i == 0)
    def _():
        for j in range(EO):
            ga_ref[j * R : (j + 1) * R, :] = weighted(a_ref[j])
        for d in range(DP):
            out_ref[d, :, DZ : DZ + FA] = ga_ref[:, d * FA : (d + 1) * FA].astype(bf16)

    for j in range(EO):
        out_ref[i, j * R : (j + 1) * R, 0:DZ] = weighted(b_ref[j]).astype(bf16)


def shape(*dims, dtype=bf16):
    return jax.ShapeDtypeStruct(dims, dtype)


def whole(*dims):
    return pl.BlockSpec(dims, lambda i: (0,) * len(dims))


def call(kernel, name, cost=1, **kw):
    return pl.pallas_call(
        kernel,
        name=name,
        compiler_params=pltpu.CompilerParams(**PARAMS),
        cost_estimate=pl.CostEstimate(flops=max(cost << 30, 1024), bytes_accessed=1024, transcendentals=0),
        **kw,
    )


def in_hbm(v):
    return pltpu.with_memory_space_constraint(v, pltpu.HBM)


def shards(grad, gates, routes, example, hidden, down, up):
    me = lax.axis_index("expert")
    group = lax.axis_index("dp")
    here = jnp.stack([me // NZ, group // 2, group % 2, me % NZ]).astype(i32)
    hidden = in_hbm(hidden[0])

    def over_y(v, k):
        pairs = [(a * NZ + b, ((a + k) % NY) * NZ + b) for a in range(NY) for b in range(NZ)]
        return lax.ppermute(v, "expert", pairs)

    def over_x(v, k):
        pairs = [(a * 2 + b, ((a + k) % 4) * 2 + b) for a in range(4) for b in range(2)]
        return lax.ppermute(v, "dp", pairs)

    def ring(v, over, *beside):
        left, right = over(v, 1), over(v, 3)
        if beside:
            left, right, *beside = lax.optimization_barrier((left, right, *beside))
        half = v.shape[0] // 2
        return [*beside, jnp.concatenate([v, left, right, over(left[:half], 1), over(right[half:], 3)])]

    part = lax.dynamic_slice_in_dim(up.reshape(EO * R, D), group * 8, 8, 0)
    part = part.reshape(8, NZ, DZ).transpose(1, 0, 2)
    part = lax.all_to_all(part, "expert", 0, 0, axis_index_groups=ZGROUPS, tiled=True)
    m1 = call(
        send_kernel, "send",
        grid=(1,),
        in_specs=[whole(TOK, D), whole(TOPK, TOK), whole(TOPK, TOK), whole(1, TOK)],
        out_specs=whole(NZ, MROWS, DZ), out_shape=shape(NZ, MROWS, DZ),
    )(*[in_hbm(v) for v in (grad[0], gates[0].T, routes[0].T, example)])

    m1, down_low = lax.optimization_barrier((m1, down))
    own = lax.all_to_all(m1, "expert", 0, 0, axis_index_groups=ZGROUPS, tiled=True)
    low = call(
        low_kernel, "low",
        grid=(EO,),
        in_specs=[
            pl.BlockSpec((1, SLOTS, F), lambda i: (i, 0, 0)),
            pl.BlockSpec((1, R, F), lambda i: (i, 0, 0)),
        ],
        out_specs=pl.BlockSpec((R, PSLOTS), lambda i: (i, 0)),
        out_shape=shape(EO * R, PSLOTS),
    )(hidden, down_low)
    low, mine = ring(*ring(part.reshape(NZ * 8, DZ), over_y), over_x, low)
    other = lax.ppermute(mine, "dp", [(g, g ^ 1) for g in range(DP)])
    mine, other = (v.reshape(4, NY, NZ * 8, DZ) for v in (mine, other))

    left = over_y(own, 1)
    right = over_y(own, NY - 1)

    def gather(cost, *blocks):
        return call(
            gather_kernel, "gather", cost,
            grid=(2,),
            in_specs=[SMEM] + [whole(*v.shape) for v in blocks],
            out_specs=[
                pl.BlockSpec((EY // 2, NZ * PCAP, DZ), lambda i: (i, 0, 0)),
                pl.BlockSpec((NZ // 2, EO, NZ * PCAP), lambda i: (i, 0, 0)),
            ],
            out_shape=[pltpu.VMEM((EY, NZ * PCAP, DZ), bf16), shape(NZ, EO, NZ * PCAP, dtype=f32)],
        )(here, *blocks)

    sent = call(
        back_kernel, "back", 60,
        in_specs=[SMEM] + [VMEM] * 3, out_specs=VMEM, out_shape=shape(NSRC, BROWS, 128),
        scratch_shapes=[
            pltpu.VMEM((DP, NY, NZ * 8, DZ), bf16),
            pltpu.VMEM((NZ, 16, DZ), f32),
        ],
    )(here, own, mine, other)
    back = lax.all_to_all(sent, "expert", 0, 0, tiled=True)

    own, sent = lax.optimization_barrier((own, sent))

    def over_z(v, k):
        pairs = [(a * NZ + b, a * NZ + (b + k) % NZ) for a in range(NY) for b in range(NZ)]
        return lax.ppermute(v, "expert", pairs)

    part_own = gather(0, own)
    right, left, part_own, low = lax.optimization_barrier((right, left, part_own, low))
    far0 = over_y(left[: NZ // 2], 1)
    far1 = over_y(right[NZ // 2 :], NY - 1)
    near = [over_z(low, 1), over_z(low, NZ - 1)]
    lows = [
        jnp.concatenate([low, *near]),
        over_z(jnp.concatenate([low, *near]), 3),
        over_z(jnp.concatenate([low, near[0]]), NZ - 3),
    ]
    part_right, part_left = gather(80, right), gather(0, left)
    back, part_right, part_left = lax.optimization_barrier((back, part_right, part_left))
    slots, big_a, sq_a = call(
        a_kernel, "norm_a", 0,
        grid=(EO,),
        in_specs=[
            whole(NSRC, BROWS, 128),
            pl.BlockSpec((1, SLOTS, F), lambda i: (i, 0, 0)),
        ],
        out_specs=[
            pl.BlockSpec((1, R, SLOTS), lambda i: (i, 0, 0)),
            pl.BlockSpec((1, NEX * R, F), lambda i: (i, 0, 0)),
            whole(NEX * R, 128),
        ],
        out_shape=[
            shape(EO, R, SLOTS),
            shape(EO, NEX * R, F),
            shape(NEX * R, 128, dtype=f32),
        ],
        scratch_shapes=[pltpu.VMEM((2 * R, NSRC * 64), bf16)],
    )(back, hidden)

    far0, far1, sq_a = lax.optimization_barrier((far0, far1, sq_a))
    parts = [part_own, part_right, gather(1, far0, far1), part_left]
    big_b, norm = call(
        b_kernel, "norm_b",
        grid=(NZ,),
        in_specs=[SMEM]
        + [pl.BlockSpec((EO, NZ * PCAP, DZ), lambda i: (i, 0, 0))] * 4
        + [pl.BlockSpec((1, EO, NZ * PCAP), lambda i: (i, 0, 0))] * 4
        + [
            *[whole(len(v) * EO * R, PSLOTS) for v in LOWS],
            whole(NEX * R, 128),
        ],
        out_specs=[
            pl.BlockSpec((EO, NEX * R, DZ), lambda i: (i, 0, 0)),
            whole(NSRC, 8, 128),
        ],
        out_shape=[shape(EY, NEX * R, DZ), shape(NSRC, 8, 128, dtype=f32)],
        scratch_shapes=[
            pltpu.VMEM((NEX * R, 128), f32),
            pltpu.VMEM((NZ, EO * R, PSLOTS), bf16),
        ],
    )(here, *[pltpu.with_memory_space_constraint(v[0], pltpu.VMEM) for v in parts], *[v[1] for v in parts], *lows, sq_a)
    norm = lax.all_to_all(norm, "expert", 0, 0, tiled=True)

    sums = call(
        clip_kernel, "clip",
        grid=(NZ,),
        in_specs=[
            whole(NSRC, 8, 128),
            pl.BlockSpec((EO, NEX * R, DZ), lambda i: (i, 0, 0)),
            whole(EO, NEX * R, F),
        ],
        out_specs=whole(DP, EO * R, DZ + FA),
        out_shape=shape(DP, EO * R, DZ + FA),
        scratch_shapes=[pltpu.VMEM((EO * R, F), f32)],
    )(norm, big_b, big_a)
    slots, sums = lax.optimization_barrier((slots, sums))
    sums = lax.all_to_all(sums, "dp", 0, 0, tiled=True)
    hidden_grad = call(
        hidden_kernel, "hidden_grad",
        grid=(EO,),
        in_specs=[
            pl.BlockSpec((1, R, SLOTS), lambda i: (i, 0, 0)),
            pl.BlockSpec((1, R, F), lambda i: (i, 0, 0)),
        ],
        out_specs=pl.BlockSpec((1, SLOTS, F), lambda i: (i, 0, 0)),
        out_shape=shape(EO, SLOTS, F),
    )(slots, down)
    sums, hidden_grad = lax.optimization_barrier((sums, hidden_grad))
    sums = jnp.sum(sums.astype(f32), axis=0)
    swap = [
        ((g * NY + a) * NZ + b, (b * NY + a) * NZ + g)
        for g in range(DP) for a in range(NY) for b in range(NZ)
    ]
    grad_b = lax.ppermute(sums[:, :DZ].astype(bf16), ("dp", "expert"), swap).astype(f32)
    return (
        hidden_grad[None],
        sums[:, DZ:].reshape(EO, R, FA),
        grad_b.reshape(EO, R, DZ),
    )


def solution(mesh):
    return jax.shard_map(
        shards,
        mesh=mesh,
        in_specs=(
            P("dp", "expert", None),
            P("dp", "expert", None),
            P("dp", "expert", None),
            P("dp", "expert"),
            P("dp", "expert", None, None),
            P("expert", None, None),
            P("expert", None, None),
        ),
        out_specs=(P("dp", "expert", None, None), P("expert", None, "dp"), P("expert", None, "dp")),
        check_vma=False,
    )
```

```python
import math

import jax
import jax.numpy as jnp
from jax import lax
from jax.experimental import pallas as pl
from jax.experimental.pallas import tpu as pltpu
from jax.sharding import PartitionSpec as P

NY, NZ, DP = 4, 8, 8
NSRC = NY * NZ
TOK = 128
TOPK = 8
D = 4096
DZ = D // NZ
F = 1536
R = 16
EXP = 128
EO = 4
EY = EXP // NY
CAP = 12
PCAP = 16
SLOTS = NSRC * CAP
PSLOTS = NSRC * PCAP
NEX = 16
MROWS = TOK + 16
SCALE = 2.0
GAMMA = 0.01
FA = F // DP
f32 = jnp.float32
bf16 = jnp.bfloat16
i32 = jnp.int32

ZGROUPS = [[y * NZ + z for z in range(NZ)] for y in range(NY)]
RING = (0, 3, 1, 2)
LOWS = ((0, -1, 1), (-3, -4, -2), (3, 2))
HALF = EY * PCAP // 2
BROWS = EO * R + 16
VMEM = pl.BlockSpec(memory_space=pltpu.VMEM)
SMEM = pl.BlockSpec(memory_space=pltpu.SMEM)
PARAMS = dict(vmem_limit_bytes=14 * 1024 * 1024)


def dot(a, b, ca=1, cb=0):
    return lax.dot_general(a, b, (((ca,), (cb,)), ((), ())), preferred_element_type=f32)


def iota(shape, dim):
    return lax.broadcasted_iota(i32, shape, dim)


def pad_matrix():
    lane = iota((SLOTS, PSLOTS), 1)
    s = lane & (PCAP - 1)
    at = (lane >> 4) * CAP + s
    return jnp.where((at == iota((SLOTS, PSLOTS), 0)) & (s < CAP), 1.0, 0.0).astype(bf16)


def send_kernel(x_ref, gate_ref, route_ref, example_ref, out_ref):
    gate_of = gate_ref[...].T
    route_of = route_ref[...].astype(f32).T.astype(i32)
    expert = iota((TOK, EXP), 1)
    routed = jnp.zeros((TOK, EXP), f32)
    gate = jnp.zeros((TOK, EXP), f32)
    for k in range(TOPK):
        hit = route_of[:, k : k + 1] == expert
        routed = jnp.where(hit, 1.0, routed)
        gate = jnp.where(hit, gate_of[:, k : k + 1], gate)
    before = jnp.where(iota((TOK, TOK), 1) < iota((TOK, TOK), 0), 1.0, 0.0).astype(bf16)
    rank = jnp.where(routed > 0.5, dot(before, routed.astype(bf16)), 64.0).astype(bf16)
    high = gate.astype(bf16)
    low = (gate - high.astype(f32)).astype(bf16)
    row = iota((16, TOK), 0)
    ids = jnp.where(
        row == 0,
        iota((16, TOK), 1) + 1,
        jnp.where(row == 1, jnp.broadcast_to(example_ref[...], (16, TOK)) + 1, 0),
    ).astype(f32).astype(bf16)
    ones = jnp.ones((16, TOK), bf16)
    toks, highs, lows, labels = [], [], [], []
    for y in range(NY):
        lane = iota((EXP, EY * PCAP), 1)
        expand = jnp.where((lane >> 4) + y * EY == iota((EXP, EY * PCAP), 0), 1.0, 0.0).astype(bf16)
        place = (iota((TOK, EY * PCAP), 1) & (PCAP - 1)).astype(f32)
        here = dot(rank, expand) == place
        tab = dot(ids, jnp.where(here, 1.0, 0.0).astype(bf16))
        toks.append(tab[0:1])
        labels.append(tab[1:2])
        highs.append(dot(ones, jnp.where(here, dot(high, expand), 0.0).astype(bf16))[0:1])
        lows.append(dot(ones, jnp.where(here, dot(low, expand), 0.0).astype(bf16))[0:1])
    table = jnp.concatenate(toks + highs + lows + labels, axis=0).astype(bf16)
    for z in range(NZ):
        out_ref[z, 0:TOK, :] = x_ref[:, z * DZ : (z + 1) * DZ]
        out_ref[z, TOK:MROWS, :] = table


def low_kernel(hidden_ref, down_ref, out_ref):
    low = dot(down_ref[0], hidden_ref[0], 1, 1).astype(bf16)
    low = dot(low, pad_matrix()).astype(bf16)
    out_ref[...] = low


def gather_kernel(y_ref, *refs):
    blocks, (rows_ref, label_ref) = refs[:-2], refs[-2:]
    y = y_ref[0]
    lanes = pl.ds(pl.multiple_of(pl.program_id(0) * HALF, HALF), HALF)
    row = iota((16, HALF), 0)
    token = iota((HALF, TOK), 1) + 1
    lane = iota((EY // 2, HALF), 1)
    expert = iota((EY // 2, HALF), 0)
    labels = jnp.zeros((EY // 2, NZ * PCAP), f32)
    q = 0
    for block_ref in blocks:
        for i in range(block_ref.shape[0]):
            x = block_ref[i, 0:TOK, :]
            table = block_ref[i, TOK:MROWS, lanes].astype(f32)

            def pick(k):
                return jnp.sum(jnp.where(row == 4 * k + y, table, 0.0), axis=0, keepdims=True)

            tok, high, low, label = pick(0), pick(1), pick(2), pick(3)
            here = jnp.where(lane >> 4 == expert, label, 0.0).astype(bf16)
            at = (iota((HALF, NZ * PCAP), 0) & (PCAP - 1)) + q * PCAP
            move = jnp.where(at == iota((HALF, NZ * PCAP), 1), 1.0, 0.0).astype(bf16)
            labels = labels + dot(here, move)
            cols = jnp.concatenate([tok, high, low, jnp.zeros((5, HALF), f32)], axis=0).T
            here = cols[:, 0:1].astype(i32) == token
            place = jnp.concatenate(
                [
                    jnp.where(here, cols[:, 1:2], 0.0).astype(bf16),
                    jnp.where(here, cols[:, 2:3], 0.0).astype(bf16),
                ],
                axis=1,
            )
            rows = dot(place, jnp.concatenate([x, x], axis=0)).astype(bf16)
            rows_ref[:, q * PCAP : (q + 1) * PCAP, :] = rows.reshape(EY // 2, PCAP, DZ)
            q += 1
    for i in range(NZ // 2):
        label_ref[i] = labels[i * EO : (i + 1) * EO]


def back_kernel(at_ref, own_ref, mine_ref, other_ref, out_ref, up_ref, table_ref):
    me_y, me_x, me_core = at_ref[0], at_ref[1], at_ref[2]
    token = (iota((TOK, 256), 0) + 1).astype(f32)
    group = iota((R, 256), 1) >> 4
    first = iota((R, 128), 1) < 64
    for k in range(NY):
        g = ((me_x + RING[k]) & 3) * 2
        up_ref[g + me_core] = mine_ref[k]
        up_ref[g + 1 - me_core] = other_ref[k]
    for q in range(NZ):
        table_ref[q] = own_ref[q, TOK:MROWS, :].astype(f32)

    def pair(p, carry):
        x = jnp.concatenate([own_ref[2 * p, 0:TOK, :], own_ref[2 * p + 1, 0:TOK, :]], axis=0)
        at = pl.multiple_of(p * R, R)
        for k in range(NY):
            y = (me_y + RING[k]) & 3
            up = jnp.concatenate([up_ref[g, k] for g in range(DP)], axis=0)
            dense = dot(up, x, 1, 1)
            dense = jnp.concatenate(
                [dense[g * 64 + zo * 8 : g * 64 + zo * 8 + 8] for zo in range(NZ) for g in range(DP)],
                axis=0,
            )
            high = dense.astype(bf16)
            low = (dense - high.astype(f32)).astype(bf16)
            for c in range(2):
                found = []
                for h in range(2):
                    def entry(kind):
                        return table_ref[2 * p + h, pl.ds(4 * kind + y, 1), c * 256 : (c + 1) * 256]

                    place = jnp.where(entry(0) == token, 1.0, 0.0).astype(bf16)
                    part = dot(
                        jnp.concatenate(
                            [
                                v[c * 256 : (c + 1) * 256, h * TOK : (h + 1) * TOK]
                                for v in (high, low)
                            ],
                            axis=1,
                        ),
                        jnp.concatenate([place, place], axis=0),
                    )
                    total = jnp.where(group == 0, part[0:R], 0.0)
                    for e in range(1, 16):
                        total = jnp.where(group == e, part[e * R : (e + 1) * R], total)
                    found.append(total * (entry(1) + entry(2)))
                for t in range(2):
                    a, b = (v[:, t * 128 : (t + 1) * 128] for v in found)
                    o = y * NZ + c * 4 + t * 2
                    out_ref[o, pl.ds(at, R), :] = jnp.where(first, a, pltpu.roll(b, 64, 1)).astype(bf16)
                    out_ref[o + 1, pl.ds(at, R), :] = jnp.where(first, pltpu.roll(a, 64, 1), b).astype(bf16)
        return carry

    lax.fori_loop(0, NZ // 2, pair, 0, unroll=True)

    half = iota((NZ, 128), 1) < 64
    pad = jnp.zeros((8, 128), f32)
    for y in range(NY):
        def label(h):
            rows = [table_ref[2 * p + h, 12 + y : 13 + y, :] for p in range(NZ // 2)]
            return jnp.concatenate(rows + [jnp.zeros((4, DZ), f32)], axis=0)

        even, odd = label(0), label(1)
        for t in range(4):
            a, b = even[:, t * 128 : (t + 1) * 128], odd[:, t * 128 : (t + 1) * 128]
            o = y * NZ + t * 2
            for i, v in enumerate(
                (jnp.where(half, a, pltpu.roll(b, 64, 1)), jnp.where(half, pltpu.roll(a, 64, 1), b))
            ):
                out_ref[o + i, EO * R : EO * R + 16, :] = jnp.concatenate([v, pad], axis=0).astype(bf16)


def squares(v):
    v = v * v
    total = v[:, 0:128]
    for c in range(1, v.shape[1] // 128):
        total = total + v[:, c * 128 : (c + 1) * 128]
    return total


def spread(label, value):
    label = jnp.broadcast_to(label, value.shape).astype(bf16)
    value = value.astype(bf16)
    return jnp.concatenate(
        [jnp.where(label == n + 1.0, value, jnp.zeros_like(value)) for n in range(NEX)], axis=0
    )


def b_kernel(y_ref, own, right, far, left, lab0, lab1, lab2, lab3, *refs):
    low_refs, (sqa_ref, out_ref, norm_ref, sq_ref, low_ref) = refs[:3], refs[3:]
    i = pl.program_id(0)
    y = y_ref[0]

    @pl.when(i == 0)
    def _():
        sq_ref[...] = sqa_ref[...]
        for ref, places in zip(low_refs, LOWS):
            for n, k in enumerate(places):
                low_ref[(y_ref[3] + k) & (NZ - 1)] = ref[n * EO * R : (n + 1) * EO * R, :]

    total = jnp.zeros((NEX * R, 128), f32)
    for j in range(EO):
        label = jnp.concatenate([v[0, j : j + 1, :] for v in (lab0, lab1, lab2, lab3)], axis=1)
        low = jnp.concatenate(
            [
                low_ref[i, j * R : (j + 1) * R, pl.ds(pl.multiple_of(((y + k) & 3) * 128, 128), 128)]
                for k in range(NY)
            ],
            axis=1,
        )
        rows = jnp.concatenate([own[j], right[j], far[j], left[j]], axis=0)
        b = dot(spread(label, low), rows)
        total = total + squares(b)
        out_ref[j] = b.astype(bf16)
    sq_ref[...] += total

    @pl.when(i == NZ - 1)
    def _():
        s = jnp.sum(sq_ref[...].reshape(NEX, R, 128), axis=1)
        s = jnp.broadcast_to(jnp.sum(s, axis=1, keepdims=True), (NEX, 128)) * (SCALE * SCALE)
        s = jnp.where(iota((8, 128), 1) < 64, s[0:8], s[8:16])
        norm_ref[...] = jnp.broadcast_to(s[None], norm_ref.shape)


def a_kernel(back_ref, hidden_ref, slots_ref, a_ref, sq_ref, total_ref):
    j = pl.program_id(0)

    @pl.when(j == 0)
    def _():
        sq_ref[...] = jnp.zeros_like(sq_ref)
        for k in range(NY):
            total = back_ref[k * NZ, 0 : EO * R, :].astype(f32)
            for z in range(1, NZ):
                total = total + back_ref[k * NZ + z, 0 : EO * R, :].astype(f32)
            labels = back_ref[k * NZ, EO * R : BROWS, :].astype(f32)
            for p in range(NZ // 2):
                at = (k * 4 + p) * 128
                total_ref[0:R, at : at + 128] = total[p * R : (p + 1) * R].astype(bf16)
                total_ref[R : 2 * R, at : at + 128] = jnp.broadcast_to(
                    labels[p : p + 1], (R, 128)
                ).astype(bf16)

    tiles = []
    for c in range(3):
        lane = iota((768, 128), 0) + c * 640
        s = lane & (PCAP - 1)
        at = jnp.where(((lane >> 4) & 3 == j) & (s < CAP), (lane >> 6) * CAP + s, -1)
        pick = jnp.where(at == iota((768, 128), 1) + c * 128, 1.0, 0.0).astype(bf16)
        tiles.append(dot(total_ref[:, c * 640 : c * 640 + 768], pick))
    tiles = jnp.concatenate(tiles, axis=1)
    back, label = tiles[0:R], tiles[R : R + 1]
    a = dot(spread(label, back), hidden_ref[0])
    sq_ref[...] += squares(a)
    a_ref[0] = a.astype(bf16)
    slots_ref[0] = back.astype(bf16)


def hidden_kernel(slots_ref, down_ref, grad_ref):
    grad_ref[0] = (SCALE * dot(slots_ref[0], down_ref[0], 0, 0)).astype(bf16)


def clip_kernel(norm_ref, b_ref, a_ref, out_ref, ga_ref):
    i = pl.program_id(0)
    radius = math.sqrt(EXP * R * (D + F) / (DP * NEX))
    norm = norm_ref[0]
    for q in range(1, NSRC):
        norm = norm + norm_ref[q]
    other = pltpu.roll(norm, 64, 1)
    first = iota((8, 128), 1) < 64
    norm = jnp.concatenate(
        [jnp.where(first, norm, other), jnp.where(first, other, norm)], axis=0
    )
    factor = SCALE * radius / (jnp.sqrt(norm) + GAMMA)
    wide = jnp.concatenate([factor, factor], axis=1)
    column = iota((NEX, NEX * R), 1)
    wide = jnp.sum(jnp.where(column >> 4 == iota((NEX, NEX * R), 0), wide, 0.0), axis=0, keepdims=True)
    wide = jnp.where(column & 15 == iota((R, NEX * R), 0), wide, 0.0)
    high = wide.astype(bf16)
    pick = jnp.concatenate([high, (wide - high.astype(f32)).astype(bf16)], axis=0)

    def weighted(v):
        v = dot(pick, v)
        return v[0:R] + v[R:]

    @pl.when(i == 0)
    def _():
        for j in range(EO):
            ga_ref[j * R : (j + 1) * R, :] = weighted(a_ref[j])
        for d in range(DP):
            out_ref[d, :, DZ : DZ + FA] = ga_ref[:, d * FA : (d + 1) * FA].astype(bf16)

    for j in range(EO):
        out_ref[i, j * R : (j + 1) * R, 0:DZ] = weighted(b_ref[j]).astype(bf16)


def shape(*dims, dtype=bf16):
    return jax.ShapeDtypeStruct(dims, dtype)


def whole(*dims):
    return pl.BlockSpec(dims, lambda i: (0,) * len(dims))


def call(kernel, name, cost=1, **kw):
    return pl.pallas_call(
        kernel,
        name=name,
        compiler_params=pltpu.CompilerParams(**PARAMS),
        cost_estimate=pl.CostEstimate(flops=max(cost << 30, 1024), bytes_accessed=1024, transcendentals=0),
        **kw,
    )


def in_hbm(v):
    return pltpu.with_memory_space_constraint(v, pltpu.HBM)


def shards(grad, gates, routes, example, hidden, down, up):
    me = lax.axis_index("expert")
    group = lax.axis_index("dp")
    here = jnp.stack([me // NZ, group // 2, group % 2, me % NZ]).astype(i32)
    hidden = in_hbm(hidden[0])

    def over_y(v, k):
        pairs = [(a * NZ + b, ((a + k) % NY) * NZ + b) for a in range(NY) for b in range(NZ)]
        return lax.ppermute(v, "expert", pairs)

    def over_x(v, k):
        pairs = [(a * 2 + b, ((a + k) % 4) * 2 + b) for a in range(4) for b in range(2)]
        return lax.ppermute(v, "dp", pairs)

    def ring(v, over, *beside):
        left, right = over(v, 1), over(v, 3)
        if beside:
            left, right, *beside = lax.optimization_barrier((left, right, *beside))
        half = v.shape[0] // 2
        return [*beside, jnp.concatenate([v, left, right, over(left[:half], 1), over(right[half:], 3)])]

    part = lax.dynamic_slice_in_dim(up.reshape(EO * R, D), group * 8, 8, 0)
    part = part.reshape(8, NZ, DZ).transpose(1, 0, 2)
    part = lax.all_to_all(part, "expert", 0, 0, axis_index_groups=ZGROUPS, tiled=True)
    m1 = call(
        send_kernel, "send",
        grid=(1,),
        in_specs=[whole(TOK, D), whole(TOPK, TOK), whole(TOPK, TOK), whole(1, TOK)],
        out_specs=whole(NZ, MROWS, DZ), out_shape=shape(NZ, MROWS, DZ),
    )(*[in_hbm(v) for v in (grad[0], gates[0].T, routes[0].T, example)])

    m1, down_low = lax.optimization_barrier((m1, down))
    own = lax.all_to_all(m1, "expert", 0, 0, axis_index_groups=ZGROUPS, tiled=True)
    low = call(
        low_kernel, "low",
        grid=(EO,),
        in_specs=[
            pl.BlockSpec((1, SLOTS, F), lambda i: (i, 0, 0)),
            pl.BlockSpec((1, R, F), lambda i: (i, 0, 0)),
        ],
        out_specs=pl.BlockSpec((R, PSLOTS), lambda i: (i, 0)),
        out_shape=shape(EO * R, PSLOTS),
    )(hidden, down_low)
    low, mine = ring(*ring(part.reshape(NZ * 8, DZ), over_y), over_x, low)

    def over_z(v, k):
        pairs = [(a * NZ + b, a * NZ + (b + k) % NZ) for a in range(NY) for b in range(NZ)]
        return lax.ppermute(v, "expert", pairs)

    near0, near1 = over_z(low, 1), over_z(low, NZ - 1)
    near0, near1, mine = lax.optimization_barrier((near0, near1, mine))
    lows = [jnp.concatenate([low, near0, near1]), jnp.concatenate([low, near0])]
    lows = [lows[0], over_z(lows[0], 3), over_z(lows[1], NZ - 3)]
    other = lax.ppermute(mine, "dp", [(g, g ^ 1) for g in range(DP)])
    mine, other = (v.reshape(4, NY, NZ * 8, DZ) for v in (mine, other))

    low_half, high_half = own[: NZ // 2], own[NZ // 2 :]
    left0, right1 = over_y(low_half, 1), over_y(high_half, NY - 1)
    left1, right0 = over_y(high_half, 1), over_y(low_half, NY - 1)
    far0, far1 = over_y(left0, 1), over_y(right1, NY - 1)

    def gather(cost, *blocks, space=pltpu.HBM):
        return call(
            gather_kernel, "gather", cost,
            grid=(2,),
            in_specs=[SMEM] + [whole(*v.shape) for v in blocks],
            out_specs=[
                pl.BlockSpec((EY // 2, NZ * PCAP, DZ), lambda i: (i, 0, 0)),
                pl.BlockSpec((NZ // 2, EO, NZ * PCAP), lambda i: (i, 0, 0)),
            ],
            out_shape=[space((EY, NZ * PCAP, DZ), bf16), shape(NZ, EO, NZ * PCAP, dtype=f32)],
        )(here, *blocks)

    sent = call(
        back_kernel, "back", 60,
        in_specs=[SMEM] + [VMEM] * 3, out_specs=VMEM, out_shape=shape(NSRC, BROWS, 128),
        scratch_shapes=[
            pltpu.VMEM((DP, NY, NZ * 8, DZ), bf16),
            pltpu.VMEM((NZ, 16, DZ), f32),
        ],
    )(here, own, mine, other)
    back = lax.all_to_all(sent, "expert", 0, 0, tiled=True)

    own, sent, *lows = lax.optimization_barrier((own, sent, *lows))

    def over_z(v, k):
        pairs = [(a * NZ + b, a * NZ + (b + k) % NZ) for a in range(NY) for b in range(NZ)]
        return lax.ppermute(v, "expert", pairs)

    part_own = gather(0, own)
    left0, left1, right0, right1, part_own = lax.optimization_barrier(
        (left0, left1, right0, right1, part_own)
    )
    part_right, part_left = gather(80, right0, right1), gather(0, left0, left1)
    back, part_right, part_left = lax.optimization_barrier((back, part_right, part_left))
    slots, big_a, sq_a = call(
        a_kernel, "norm_a", 0,
        grid=(EO,),
        in_specs=[
            whole(NSRC, BROWS, 128),
            pl.BlockSpec((1, SLOTS, F), lambda i: (i, 0, 0)),
        ],
        out_specs=[
            pl.BlockSpec((1, R, SLOTS), lambda i: (i, 0, 0)),
            pl.BlockSpec((1, NEX * R, F), lambda i: (i, 0, 0)),
            whole(NEX * R, 128),
        ],
        out_shape=[
            shape(EO, R, SLOTS),
            shape(EO, NEX * R, F),
            shape(NEX * R, 128, dtype=f32),
        ],
        scratch_shapes=[pltpu.VMEM((2 * R, NSRC * 64), bf16)],
    )(back, hidden)

    far0, far1, sq_a = lax.optimization_barrier((far0, far1, sq_a))
    parts = [part_own, part_right, gather(0, far0, far1, space=pltpu.VMEM), part_left]
    big_b, norm = call(
        b_kernel, "norm_b",
        grid=(NZ,),
        in_specs=[SMEM]
        + [pl.BlockSpec((EO, NZ * PCAP, DZ), lambda i: (i, 0, 0))] * 4
        + [pl.BlockSpec((1, EO, NZ * PCAP), lambda i: (i, 0, 0))] * 4
        + [
            *[whole(len(v) * EO * R, PSLOTS) for v in LOWS],
            whole(NEX * R, 128),
        ],
        out_specs=[
            pl.BlockSpec((EO, NEX * R, DZ), lambda i: (i, 0, 0)),
            whole(NSRC, 8, 128),
        ],
        out_shape=[shape(EY, NEX * R, DZ), shape(NSRC, 8, 128, dtype=f32)],
        scratch_shapes=[
            pltpu.VMEM((NEX * R, 128), f32),
            pltpu.VMEM((NZ, EO * R, PSLOTS), bf16),
        ],
    )(here, *[
            pltpu.with_memory_space_constraint(v[0], pltpu.VMEM if n == 2 else pltpu.HBM)
            for n, v in enumerate(parts)
        ], *[v[1] for v in parts], *lows, sq_a)
    norm = lax.all_to_all(norm, "expert", 0, 0, tiled=True)

    sums = call(
        clip_kernel, "clip",
        grid=(NZ,),
        in_specs=[
            whole(NSRC, 8, 128),
            pl.BlockSpec((EO, NEX * R, DZ), lambda i: (i, 0, 0)),
            whole(EO, NEX * R, F),
        ],
        out_specs=whole(DP, EO * R, DZ + FA),
        out_shape=shape(DP, EO * R, DZ + FA),
        scratch_shapes=[pltpu.VMEM((EO * R, F), f32)],
    )(norm, big_b, big_a)
    slots, sums = lax.optimization_barrier((slots, sums))
    sums = lax.all_to_all(sums, "dp", 0, 0, tiled=True)
    hidden_grad = call(
        hidden_kernel, "hidden_grad",
        grid=(EO,),
        in_specs=[
            pl.BlockSpec((1, R, SLOTS), lambda i: (i, 0, 0)),
            pl.BlockSpec((1, R, F), lambda i: (i, 0, 0)),
        ],
        out_specs=pl.BlockSpec((1, SLOTS, F), lambda i: (i, 0, 0)),
        out_shape=shape(EO, SLOTS, F),
    )(slots, down)
    sums, hidden_grad = lax.optimization_barrier((sums, hidden_grad))
    sums = jnp.sum(sums.astype(f32), axis=0)
    swap = [
        ((g * NY + a) * NZ + b, (b * NY + a) * NZ + g)
        for g in range(DP) for a in range(NY) for b in range(NZ)
    ]
    grad_b = lax.ppermute(sums[:, :DZ].astype(bf16), ("dp", "expert"), swap).astype(f32)
    return (
        hidden_grad[None],
        sums[:, DZ:].reshape(EO, R, FA),
        grad_b.reshape(EO, R, DZ),
    )


def solution(mesh):
    return jax.shard_map(
        shards,
        mesh=mesh,
        in_specs=(
            P("dp", "expert", None),
            P("dp", "expert", None),
            P("dp", "expert", None),
            P("dp", "expert"),
            P("dp", "expert", None, None),
            P("expert", None, None),
            P("expert", None, None),
        ),
        out_specs=(P("dp", "expert", None, None), P("expert", None, "dp"), P("expert", None, "dp")),
        check_vma=False,
    )
```

```python
import math

import jax
import jax.numpy as jnp
from jax import lax
from jax.experimental import pallas as pl
from jax.experimental.pallas import tpu as pltpu
from jax.sharding import PartitionSpec as P

NY, NZ, DP = 4, 8, 8
NSRC = NY * NZ
TOK = 128
TOPK = 8
D = 4096
DZ = D // NZ
F = 1536
R = 16
EXP = 128
EO = 4
EY = EXP // NY
CAP = 12
PCAP = 16
SLOTS = NSRC * CAP
PSLOTS = NSRC * PCAP
NEX = 16
MROWS = TOK + 16
SCALE = 2.0
GAMMA = 0.01
FA = F // DP
f32 = jnp.float32
bf16 = jnp.bfloat16
i32 = jnp.int32

ZGROUPS = [[y * NZ + z for z in range(NZ)] for y in range(NY)]
RING = (0, 3, 1, 2)
LOWS = ((0, -1, 1), (-3, -4, -2), (3, 2))
HALF = EY * PCAP // 2
BROWS = EO * R + 16
VMEM = pl.BlockSpec(memory_space=pltpu.VMEM)
SMEM = pl.BlockSpec(memory_space=pltpu.SMEM)
PARAMS = dict(vmem_limit_bytes=14 * 1024 * 1024)


def dot(a, b, ca=1, cb=0):
    return lax.dot_general(a, b, (((ca,), (cb,)), ((), ())), preferred_element_type=f32)


def iota(shape, dim):
    return lax.broadcasted_iota(i32, shape, dim)


def pad_matrix():
    lane = iota((SLOTS, PSLOTS), 1)
    s = lane & (PCAP - 1)
    at = (lane >> 4) * CAP + s
    return jnp.where((at == iota((SLOTS, PSLOTS), 0)) & (s < CAP), 1.0, 0.0).astype(bf16)


def send_kernel(x_ref, gate_ref, route_ref, example_ref, out_ref):
    gate_of = gate_ref[...].T
    route_of = route_ref[...].astype(f32).T.astype(i32)
    expert = iota((TOK, EXP), 1)
    routed = jnp.zeros((TOK, EXP), f32)
    gate = jnp.zeros((TOK, EXP), f32)
    for k in range(TOPK):
        hit = route_of[:, k : k + 1] == expert
        routed = jnp.where(hit, 1.0, routed)
        gate = jnp.where(hit, gate_of[:, k : k + 1], gate)
    before = jnp.where(iota((TOK, TOK), 1) < iota((TOK, TOK), 0), 1.0, 0.0).astype(bf16)
    rank = jnp.where(routed > 0.5, dot(before, routed.astype(bf16)), 64.0).astype(bf16)
    high = gate.astype(bf16)
    low = (gate - high.astype(f32)).astype(bf16)
    row = iota((16, TOK), 0)
    ids = jnp.where(
        row == 0,
        iota((16, TOK), 1) + 1,
        jnp.where(row == 1, jnp.broadcast_to(example_ref[...], (16, TOK)) + 1, 0),
    ).astype(f32).astype(bf16)
    ones = jnp.ones((16, TOK), bf16)
    toks, highs, lows, labels = [], [], [], []
    for y in range(NY):
        lane = iota((EXP, EY * PCAP), 1)
        expand = jnp.where((lane >> 4) + y * EY == iota((EXP, EY * PCAP), 0), 1.0, 0.0).astype(bf16)
        place = (iota((TOK, EY * PCAP), 1) & (PCAP - 1)).astype(f32)
        here = dot(rank, expand) == place
        tab = dot(ids, jnp.where(here, 1.0, 0.0).astype(bf16))
        toks.append(tab[0:1])
        labels.append(tab[1:2])
        highs.append(dot(ones, jnp.where(here, dot(high, expand), 0.0).astype(bf16))[0:1])
        lows.append(dot(ones, jnp.where(here, dot(low, expand), 0.0).astype(bf16))[0:1])
    table = jnp.concatenate(toks + highs + lows + labels, axis=0).astype(bf16)
    for z in range(NZ):
        out_ref[z, 0:TOK, :] = x_ref[:, z * DZ : (z + 1) * DZ]
        out_ref[z, TOK:MROWS, :] = table


def low_kernel(hidden_ref, down_ref, out_ref):
    low = dot(down_ref[0], hidden_ref[0], 1, 1).astype(bf16)
    low = dot(low, pad_matrix()).astype(bf16)
    out_ref[...] = low


def gather_kernel(y_ref, *refs):
    blocks, (rows_ref, label_ref) = refs[:-2], refs[-2:]
    y = y_ref[0]
    lanes = pl.ds(pl.multiple_of(pl.program_id(0) * HALF, HALF), HALF)
    row = iota((16, HALF), 0)
    token = iota((HALF, TOK), 1) + 1
    lane = iota((EY // 2, HALF), 1)
    expert = iota((EY // 2, HALF), 0)
    labels = jnp.zeros((EY // 2, NZ * PCAP), f32)
    q = 0
    for block_ref in blocks:
        for i in range(block_ref.shape[0]):
            x = block_ref[i, 0:TOK, :]
            table = block_ref[i, TOK:MROWS, lanes].astype(f32)

            def pick(k):
                return jnp.sum(jnp.where(row == 4 * k + y, table, 0.0), axis=0, keepdims=True)

            tok, high, low, label = pick(0), pick(1), pick(2), pick(3)
            here = jnp.where(lane >> 4 == expert, label, 0.0).astype(bf16)
            at = (iota((HALF, NZ * PCAP), 0) & (PCAP - 1)) + q * PCAP
            move = jnp.where(at == iota((HALF, NZ * PCAP), 1), 1.0, 0.0).astype(bf16)
            labels = labels + dot(here, move)
            cols = jnp.concatenate([tok, high, low, jnp.zeros((5, HALF), f32)], axis=0).T
            here = cols[:, 0:1].astype(i32) == token
            place = jnp.concatenate(
                [
                    jnp.where(here, cols[:, 1:2], 0.0).astype(bf16),
                    jnp.where(here, cols[:, 2:3], 0.0).astype(bf16),
                ],
                axis=1,
            )
            rows = dot(place, jnp.concatenate([x, x], axis=0)).astype(bf16)
            rows_ref[:, q * PCAP : (q + 1) * PCAP, :] = rows.reshape(EY // 2, PCAP, DZ)
            q += 1
    for i in range(NZ // 2):
        label_ref[i] = labels[i * EO : (i + 1) * EO]


def back_kernel(at_ref, own_ref, mine_ref, other_ref, out_ref, up_ref, table_ref):
    me_y, me_x, me_core = at_ref[0], at_ref[1], at_ref[2]
    token = (iota((TOK, 256), 0) + 1).astype(f32)
    group = iota((R, 256), 1) >> 4
    first = iota((R, 128), 1) < 64
    for k in range(NY):
        g = ((me_x + RING[k]) & 3) * 2
        up_ref[g + me_core] = mine_ref[k]
        up_ref[g + 1 - me_core] = other_ref[k]
    for q in range(NZ):
        table_ref[q] = own_ref[q, TOK:MROWS, :].astype(f32)

    def pair(p, carry):
        x = jnp.concatenate([own_ref[2 * p, 0:TOK, :], own_ref[2 * p + 1, 0:TOK, :]], axis=0)
        at = pl.multiple_of(p * R, R)
        for k in range(NY):
            y = (me_y + RING[k]) & 3
            up = jnp.concatenate([up_ref[g, k] for g in range(DP)], axis=0)
            dense = dot(up, x, 1, 1)
            dense = jnp.concatenate(
                [dense[g * 64 + zo * 8 : g * 64 + zo * 8 + 8] for zo in range(NZ) for g in range(DP)],
                axis=0,
            )
            high = dense.astype(bf16)
            low = (dense - high.astype(f32)).astype(bf16)
            for c in range(2):
                found = []
                for h in range(2):
                    def entry(kind):
                        return table_ref[2 * p + h, pl.ds(4 * kind + y, 1), c * 256 : (c + 1) * 256]

                    place = jnp.where(entry(0) == token, 1.0, 0.0).astype(bf16)
                    part = dot(
                        jnp.concatenate(
                            [
                                v[c * 256 : (c + 1) * 256, h * TOK : (h + 1) * TOK]
                                for v in (high, low)
                            ],
                            axis=1,
                        ),
                        jnp.concatenate([place, place], axis=0),
                    )
                    total = jnp.where(group == 0, part[0:R], 0.0)
                    for e in range(1, 16):
                        total = jnp.where(group == e, part[e * R : (e + 1) * R], total)
                    found.append(total * (entry(1) + entry(2)))
                for t in range(2):
                    a, b = (v[:, t * 128 : (t + 1) * 128] for v in found)
                    o = y * NZ + c * 4 + t * 2
                    out_ref[o, pl.ds(at, R), :] = jnp.where(first, a, pltpu.roll(b, 64, 1)).astype(bf16)
                    out_ref[o + 1, pl.ds(at, R), :] = jnp.where(first, pltpu.roll(a, 64, 1), b).astype(bf16)
        return carry

    lax.fori_loop(0, NZ // 2, pair, 0, unroll=True)

    half = iota((NZ, 128), 1) < 64
    pad = jnp.zeros((8, 128), f32)
    for y in range(NY):
        def label(h):
            rows = [table_ref[2 * p + h, 12 + y : 13 + y, :] for p in range(NZ // 2)]
            return jnp.concatenate(rows + [jnp.zeros((4, DZ), f32)], axis=0)

        even, odd = label(0), label(1)
        for t in range(4):
            a, b = even[:, t * 128 : (t + 1) * 128], odd[:, t * 128 : (t + 1) * 128]
            o = y * NZ + t * 2
            for i, v in enumerate(
                (jnp.where(half, a, pltpu.roll(b, 64, 1)), jnp.where(half, pltpu.roll(a, 64, 1), b))
            ):
                out_ref[o + i, EO * R : EO * R + 16, :] = jnp.concatenate([v, pad], axis=0).astype(bf16)


def squares(v):
    v = v * v
    total = v[:, 0:128]
    for c in range(1, v.shape[1] // 128):
        total = total + v[:, c * 128 : (c + 1) * 128]
    return total


def spread(label, value):
    label = jnp.broadcast_to(label, value.shape).astype(bf16)
    value = value.astype(bf16)
    return jnp.concatenate(
        [jnp.where(label == n + 1.0, value, jnp.zeros_like(value)) for n in range(NEX)], axis=0
    )


def b_kernel(y_ref, own, right, far, left, lab0, lab1, lab2, lab3, *refs):
    low_refs, (sqa_ref, out_ref, norm_ref, sq_ref, low_ref) = refs[:3], refs[3:]
    i = pl.program_id(0)
    y = y_ref[0]

    @pl.when(i == 0)
    def _():
        sq_ref[...] = sqa_ref[...]
        for ref, places in zip(low_refs, LOWS):
            for n, k in enumerate(places):
                low_ref[(y_ref[3] + k) & (NZ - 1)] = ref[n * EO * R : (n + 1) * EO * R, :]

    total = jnp.zeros((NEX * R, 128), f32)
    for j in range(EO):
        label = jnp.concatenate([v[0, j : j + 1, :] for v in (lab0, lab1, lab2, lab3)], axis=1)
        low = jnp.concatenate(
            [
                low_ref[i, j * R : (j + 1) * R, pl.ds(pl.multiple_of(((y + k) & 3) * 128, 128), 128)]
                for k in range(NY)
            ],
            axis=1,
        )
        rows = jnp.concatenate([own[j], right[j], far[j], left[j]], axis=0)
        b = dot(spread(label, low), rows)
        total = total + squares(b)
        out_ref[j] = b.astype(bf16)
    sq_ref[...] += total

    @pl.when(i == NZ - 1)
    def _():
        s = jnp.sum(sq_ref[...].reshape(NEX, R, 128), axis=1)
        s = jnp.broadcast_to(jnp.sum(s, axis=1, keepdims=True), (NEX, 128)) * (SCALE * SCALE)
        s = jnp.where(iota((NEX, 128), 1) >> 3 == iota((NEX, 128), 0), s, 0.0)
        norm_ref[...] = jnp.broadcast_to(jnp.sum(s, axis=0, keepdims=True), norm_ref.shape)


def a_kernel(back_ref, hidden_ref, slots_ref, a_ref, sq_ref, total_ref):
    j = pl.program_id(0)

    @pl.when(j == 0)
    def _():
        sq_ref[...] = jnp.zeros_like(sq_ref)
        for k in range(NY):
            total = back_ref[k * NZ, 0 : EO * R, :].astype(f32)
            for z in range(1, NZ):
                total = total + back_ref[k * NZ + z, 0 : EO * R, :].astype(f32)
            labels = back_ref[k * NZ, EO * R : BROWS, :].astype(f32)
            for p in range(NZ // 2):
                at = (k * 4 + p) * 128
                total_ref[0:R, at : at + 128] = total[p * R : (p + 1) * R].astype(bf16)
                total_ref[R : 2 * R, at : at + 128] = jnp.broadcast_to(
                    labels[p : p + 1], (R, 128)
                ).astype(bf16)

    tiles = []
    for c in range(3):
        lane = iota((768, 128), 0) + c * 640
        s = lane & (PCAP - 1)
        at = jnp.where(((lane >> 4) & 3 == j) & (s < CAP), (lane >> 6) * CAP + s, -1)
        pick = jnp.where(at == iota((768, 128), 1) + c * 128, 1.0, 0.0).astype(bf16)
        tiles.append(dot(total_ref[:, c * 640 : c * 640 + 768], pick))
    tiles = jnp.concatenate(tiles, axis=1)
    back, label = tiles[0:R], tiles[R : R + 1]
    a = dot(spread(label, back), hidden_ref[0])
    sq_ref[...] += squares(a)
    a_ref[0] = a.astype(bf16)
    slots_ref[0] = back.astype(bf16)


def hidden_kernel(slots_ref, down_ref, grad_ref):
    grad_ref[0] = (SCALE * dot(slots_ref[0], down_ref[0], 0, 0)).astype(bf16)


def clip_kernel(norm_ref, b_ref, a_ref, out_ref, ga_ref):
    i = pl.program_id(0)
    radius = math.sqrt(EXP * R * (D + F) / (DP * NEX))
    norm = jnp.sum(norm_ref[...], axis=0, keepdims=True)
    norm = jnp.where(iota((NEX, 128), 1) == iota((NEX, 128), 0) * 8, norm, 0.0)
    norm = jnp.broadcast_to(jnp.sum(norm, axis=1, keepdims=True), (NEX, 128))
    factor = SCALE * radius / (jnp.sqrt(norm) + GAMMA)
    wide = jnp.concatenate([factor, factor], axis=1)
    column = iota((NEX, NEX * R), 1)
    wide = jnp.sum(jnp.where(column >> 4 == iota((NEX, NEX * R), 0), wide, 0.0), axis=0, keepdims=True)
    wide = jnp.where(column & 15 == iota((R, NEX * R), 0), wide, 0.0)
    high = wide.astype(bf16)
    pick = jnp.concatenate([high, (wide - high.astype(f32)).astype(bf16)], axis=0)

    def weighted(v):
        v = dot(pick, v)
        return v[0:R] + v[R:]

    @pl.when(i == 0)
    def _():
        for j in range(EO):
            ga_ref[j * R : (j + 1) * R, :] = weighted(a_ref[j])
        for d in range(DP):
            out_ref[d, :, DZ : DZ + FA] = ga_ref[:, d * FA : (d + 1) * FA].astype(bf16)

    for j in range(EO):
        out_ref[i, j * R : (j + 1) * R, 0:DZ] = weighted(b_ref[j]).astype(bf16)


def shape(*dims, dtype=bf16):
    return jax.ShapeDtypeStruct(dims, dtype)


def whole(*dims):
    return pl.BlockSpec(dims, lambda i: (0,) * len(dims))


def call(kernel, name, cost=1, **kw):
    return pl.pallas_call(
        kernel,
        name=name,
        compiler_params=pltpu.CompilerParams(**PARAMS),
        cost_estimate=pl.CostEstimate(flops=max(cost << 30, 1024), bytes_accessed=1024, transcendentals=0),
        **kw,
    )


def in_hbm(v):
    return pltpu.with_memory_space_constraint(v, pltpu.HBM)


def shards(grad, gates, routes, example, hidden, down, up):
    me = lax.axis_index("expert")
    group = lax.axis_index("dp")
    here = jnp.stack([me // NZ, group // 2, group % 2, me % NZ]).astype(i32)
    hidden = in_hbm(hidden[0])

    def over_y(v, k):
        pairs = [(a * NZ + b, ((a + k) % NY) * NZ + b) for a in range(NY) for b in range(NZ)]
        return lax.ppermute(v, "expert", pairs)

    def over_x(v, k):
        pairs = [(a * 2 + b, ((a + k) % 4) * 2 + b) for a in range(4) for b in range(2)]
        return lax.ppermute(v, "dp", pairs)

    def ring(v, over, *beside):
        left, right = over(v, 1), over(v, 3)
        if beside:
            left, right, *beside = lax.optimization_barrier((left, right, *beside))
        half = v.shape[0] // 2
        return [*beside, jnp.concatenate([v, left, right, over(left[:half], 1), over(right[half:], 3)])]

    part = lax.dynamic_slice_in_dim(up.reshape(EO * R, D), group * 8, 8, 0)
    part = part.reshape(8, NZ, DZ).transpose(1, 0, 2)
    part = lax.all_to_all(part, "expert", 0, 0, axis_index_groups=ZGROUPS, tiled=True)
    m1 = call(
        send_kernel, "send",
        grid=(1,),
        in_specs=[whole(TOK, D), whole(TOPK, TOK), whole(TOPK, TOK), whole(1, TOK)],
        out_specs=whole(NZ, MROWS, DZ), out_shape=shape(NZ, MROWS, DZ),
    )(*[in_hbm(v) for v in (grad[0], gates[0].T, routes[0].T, example)])

    m1, down_low = lax.optimization_barrier((m1, down))
    own = lax.all_to_all(m1, "expert", 0, 0, axis_index_groups=ZGROUPS, tiled=True)
    low = call(
        low_kernel, "low",
        grid=(EO,),
        in_specs=[
            pl.BlockSpec((1, SLOTS, F), lambda i: (i, 0, 0)),
            pl.BlockSpec((1, R, F), lambda i: (i, 0, 0)),
        ],
        out_specs=pl.BlockSpec((R, PSLOTS), lambda i: (i, 0)),
        out_shape=shape(EO * R, PSLOTS),
    )(hidden, down_low)
    low, mine = ring(*ring(part.reshape(NZ * 8, DZ), over_y), over_x, low)

    def over_z(v, k):
        pairs = [(a * NZ + b, a * NZ + (b + k) % NZ) for a in range(NY) for b in range(NZ)]
        return lax.ppermute(v, "expert", pairs)

    near0, near1 = over_z(low, 1), over_z(low, NZ - 1)
    near0, near1, mine = lax.optimization_barrier((near0, near1, mine))
    lows = [jnp.concatenate([low, near0, near1]), jnp.concatenate([low, near0])]
    other = lax.ppermute(mine, "dp", [(g, g ^ 1) for g in range(DP)])
    mine, other = (v.reshape(4, NY, NZ * 8, DZ) for v in (mine, other))

    low_half, high_half = own[: NZ // 2], own[NZ // 2 :]
    left0, right1 = over_y(low_half, 1), over_y(high_half, NY - 1)
    left1, right0 = over_y(high_half, 1), over_y(low_half, NY - 1)

    def gather(cost, *blocks, space=pltpu.HBM):
        return call(
            gather_kernel, "gather", cost,
            grid=(2,),
            in_specs=[SMEM] + [whole(*v.shape) for v in blocks],
            out_specs=[
                pl.BlockSpec((EY // 2, NZ * PCAP, DZ), lambda i: (i, 0, 0)),
                pl.BlockSpec((NZ // 2, EO, NZ * PCAP), lambda i: (i, 0, 0)),
            ],
            out_shape=[space((EY, NZ * PCAP, DZ), bf16), shape(NZ, EO, NZ * PCAP, dtype=f32)],
        )(here, *blocks)

    sent = call(
        back_kernel, "back", 60,
        in_specs=[SMEM] + [VMEM] * 3, out_specs=VMEM, out_shape=shape(NSRC, BROWS, 128),
        scratch_shapes=[
            pltpu.VMEM((DP, NY, NZ * 8, DZ), bf16),
            pltpu.VMEM((NZ, 16, DZ), f32),
        ],
    )(here, own, mine, other)
    back = lax.all_to_all(sent, "expert", 0, 0, tiled=True)

    own, sent = lax.optimization_barrier((own, sent))

    def over_z(v, k):
        pairs = [(a * NZ + b, a * NZ + (b + k) % NZ) for a in range(NY) for b in range(NZ)]
        return lax.ppermute(v, "expert", pairs)

    part_own = gather(0, own)
    left0, left1, right0, right1, part_own, *lows = lax.optimization_barrier(
        (left0, left1, right0, right1, part_own, *lows)
    )
    far0, far1 = over_y(left0, 1), over_y(right1, NY - 1)
    lows = [lows[0], over_z(lows[0], 3), over_z(lows[1], NZ - 3)]
    part_right, part_left = gather(80, right0, right1), gather(0, left0, left1)
    back, part_right, part_left = lax.optimization_barrier((back, part_right, part_left))
    slots, big_a, sq_a = call(
        a_kernel, "norm_a", 0,
        grid=(EO,),
        in_specs=[
            whole(NSRC, BROWS, 128),
            pl.BlockSpec((1, SLOTS, F), lambda i: (i, 0, 0)),
        ],
        out_specs=[
            pl.BlockSpec((1, R, SLOTS), lambda i: (i, 0, 0)),
            pl.BlockSpec((1, NEX * R, F), lambda i: (i, 0, 0)),
            whole(NEX * R, 128),
        ],
        out_shape=[
            shape(EO, R, SLOTS),
            shape(EO, NEX * R, F),
            shape(NEX * R, 128, dtype=f32),
        ],
        scratch_shapes=[pltpu.VMEM((2 * R, NSRC * 64), bf16)],
    )(back, hidden)

    far0, far1, sq_a = lax.optimization_barrier((far0, far1, sq_a))
    parts = [part_own, part_right, gather(0, far0, far1, space=pltpu.VMEM), part_left]
    big_b, norm = call(
        b_kernel, "norm_b",
        grid=(NZ,),
        in_specs=[SMEM]
        + [pl.BlockSpec((EO, NZ * PCAP, DZ), lambda i: (i, 0, 0))] * 4
        + [pl.BlockSpec((1, EO, NZ * PCAP), lambda i: (i, 0, 0))] * 4
        + [
            *[whole(len(v) * EO * R, PSLOTS) for v in LOWS],
            whole(NEX * R, 128),
        ],
        out_specs=[
            pl.BlockSpec((EO, NEX * R, DZ), lambda i: (i, 0, 0)),
            whole(NSRC, 128),
        ],
        out_shape=[shape(EY, NEX * R, DZ), shape(NSRC, 128, dtype=f32)],
        scratch_shapes=[
            pltpu.VMEM((NEX * R, 128), f32),
            pltpu.VMEM((NZ, EO * R, PSLOTS), bf16),
        ],
    )(here, *[
            pltpu.with_memory_space_constraint(v[0], pltpu.VMEM if n == 2 else pltpu.HBM)
            for n, v in enumerate(parts)
        ], *[v[1] for v in parts], *lows, sq_a)
    norm = lax.all_to_all(norm, "expert", 0, 0, tiled=True)

    sums = call(
        clip_kernel, "clip",
        grid=(NZ,),
        in_specs=[
            whole(NSRC, 128),
            pl.BlockSpec((EO, NEX * R, DZ), lambda i: (i, 0, 0)),
            whole(EO, NEX * R, F),
        ],
        out_specs=whole(DP, EO * R, DZ + FA),
        out_shape=shape(DP, EO * R, DZ + FA),
        scratch_shapes=[pltpu.VMEM((EO * R, F), f32)],
    )(norm, big_b, big_a)
    slots, sums = lax.optimization_barrier((slots, sums))
    sums = lax.all_to_all(sums, "dp", 0, 0, tiled=True)
    hidden_grad = call(
        hidden_kernel, "hidden_grad",
        grid=(EO,),
        in_specs=[
            pl.BlockSpec((1, R, SLOTS), lambda i: (i, 0, 0)),
            pl.BlockSpec((1, R, F), lambda i: (i, 0, 0)),
        ],
        out_specs=pl.BlockSpec((1, SLOTS, F), lambda i: (i, 0, 0)),
        out_shape=shape(EO, SLOTS, F),
    )(slots, down)
    sums, hidden_grad = lax.optimization_barrier((sums, hidden_grad))
    sums = jnp.sum(sums.astype(f32), axis=0)
    swap = [
        ((g * NY + a) * NZ + b, (b * NY + a) * NZ + g)
        for g in range(DP) for a in range(NY) for b in range(NZ)
    ]
    grad_b = lax.ppermute(sums[:, :DZ].astype(bf16), ("dp", "expert"), swap).astype(f32)
    return (
        hidden_grad[None],
        sums[:, DZ:].reshape(EO, R, FA),
        grad_b.reshape(EO, R, DZ),
    )


def solution(mesh):
    return jax.shard_map(
        shards,
        mesh=mesh,
        in_specs=(
            P("dp", "expert", None),
            P("dp", "expert", None),
            P("dp", "expert", None),
            P("dp", "expert"),
            P("dp", "expert", None, None),
            P("expert", None, None),
            P("expert", None, None),
        ),
        out_specs=(P("dp", "expert", None, None), P("expert", None, "dp"), P("expert", None, "dp")),
        check_vma=False,
    )
```

```python
import math

import jax
import jax.numpy as jnp
from jax import lax
from jax.experimental import pallas as pl
from jax.experimental.pallas import tpu as pltpu
from jax.sharding import PartitionSpec as P

NY, NZ, DP = 4, 8, 8
NSRC = NY * NZ
TOK = 128
TOPK = 8
D = 4096
DZ = D // NZ
F = 1536
R = 16
EXP = 128
EO = 4
EY = EXP // NY
CAP = 12
PCAP = 16
SLOTS = NSRC * CAP
PSLOTS = NSRC * PCAP
NEX = 16
MROWS = TOK + 16
SCALE = 2.0
GAMMA = 0.01
FA = F // DP
f32 = jnp.float32
bf16 = jnp.bfloat16
i32 = jnp.int32

ZGROUPS = [[y * NZ + z for z in range(NZ)] for y in range(NY)]
RING = (0, 3, 1, 2)
LOWS = ((0, -1, 1), (-3, -4, -2), (3, 2))
HALF = EY * PCAP // 2
BROWS = EO * R + 16
VMEM = pl.BlockSpec(memory_space=pltpu.VMEM)
SMEM = pl.BlockSpec(memory_space=pltpu.SMEM)
PARAMS = dict(vmem_limit_bytes=14 * 1024 * 1024)


def dot(a, b, ca=1, cb=0):
    return lax.dot_general(a, b, (((ca,), (cb,)), ((), ())), preferred_element_type=f32)


def iota(shape, dim):
    return lax.broadcasted_iota(i32, shape, dim)


def pad_matrix():
    lane = iota((SLOTS, PSLOTS), 1)
    s = lane & (PCAP - 1)
    at = (lane >> 4) * CAP + s
    return jnp.where((at == iota((SLOTS, PSLOTS), 0)) & (s < CAP), 1.0, 0.0).astype(bf16)


def send_kernel(x_ref, gate_ref, route_ref, example_ref, out_ref):
    gate_of = gate_ref[...].T
    route_of = route_ref[...].astype(f32).T.astype(i32)
    expert = iota((TOK, EXP), 1)
    routed = jnp.zeros((TOK, EXP), f32)
    gate = jnp.zeros((TOK, EXP), f32)
    for k in range(TOPK):
        hit = route_of[:, k : k + 1] == expert
        routed = jnp.where(hit, 1.0, routed)
        gate = jnp.where(hit, gate_of[:, k : k + 1], gate)
    before = jnp.where(iota((TOK, TOK), 1) < iota((TOK, TOK), 0), 1.0, 0.0).astype(bf16)
    rank = jnp.where(routed > 0.5, dot(before, routed.astype(bf16)), 64.0).astype(bf16)
    high = gate.astype(bf16)
    low = (gate - high.astype(f32)).astype(bf16)
    row = iota((16, TOK), 0)
    ids = jnp.where(
        row == 0,
        iota((16, TOK), 1) + 1,
        jnp.where(row == 1, jnp.broadcast_to(example_ref[...], (16, TOK)) + 1, 0),
    ).astype(f32).astype(bf16)
    ones = jnp.ones((16, TOK), bf16)
    toks, highs, lows, labels = [], [], [], []
    for y in range(NY):
        lane = iota((EXP, EY * PCAP), 1)
        expand = jnp.where((lane >> 4) + y * EY == iota((EXP, EY * PCAP), 0), 1.0, 0.0).astype(bf16)
        place = (iota((TOK, EY * PCAP), 1) & (PCAP - 1)).astype(f32)
        here = dot(rank, expand) == place
        tab = dot(ids, jnp.where(here, 1.0, 0.0).astype(bf16))
        toks.append(tab[0:1])
        labels.append(tab[1:2])
        highs.append(dot(ones, jnp.where(here, dot(high, expand), 0.0).astype(bf16))[0:1])
        lows.append(dot(ones, jnp.where(here, dot(low, expand), 0.0).astype(bf16))[0:1])
    table = jnp.concatenate(toks + highs + lows + labels, axis=0).astype(bf16)
    for z in range(NZ):
        out_ref[z, 0:TOK, :] = x_ref[:, z * DZ : (z + 1) * DZ]
        out_ref[z, TOK:MROWS, :] = table


def low_kernel(hidden_ref, down_ref, out_ref):
    low = dot(down_ref[0], hidden_ref[0], 1, 1).astype(bf16)
    low = dot(low, pad_matrix()).astype(bf16)
    out_ref[...] = low


def gather_kernel(y_ref, *refs):
    blocks, (rows_ref, label_ref) = refs[:-2], refs[-2:]
    y = y_ref[0]
    lanes = pl.ds(pl.multiple_of(pl.program_id(0) * HALF, HALF), HALF)
    row = iota((16, HALF), 0)
    token = iota((HALF, TOK), 1) + 1
    lane = iota((EY // 2, HALF), 1)
    expert = iota((EY // 2, HALF), 0)
    labels = jnp.zeros((EY // 2, NZ * PCAP), f32)
    q = 0
    for block_ref in blocks:
        for i in range(block_ref.shape[0]):
            x = block_ref[i, 0:TOK, :]
            table = block_ref[i, TOK:MROWS, lanes].astype(f32)

            def pick(k):
                return jnp.sum(jnp.where(row == 4 * k + y, table, 0.0), axis=0, keepdims=True)

            tok, high, low, label = pick(0), pick(1), pick(2), pick(3)
            here = jnp.where(lane >> 4 == expert, label, 0.0).astype(bf16)
            at = (iota((HALF, NZ * PCAP), 0) & (PCAP - 1)) + q * PCAP
            move = jnp.where(at == iota((HALF, NZ * PCAP), 1), 1.0, 0.0).astype(bf16)
            labels = labels + dot(here, move)
            cols = jnp.concatenate([tok, high, low, jnp.zeros((5, HALF), f32)], axis=0).T
            here = cols[:, 0:1].astype(i32) == token
            place = jnp.concatenate(
                [
                    jnp.where(here, cols[:, 1:2], 0.0).astype(bf16),
                    jnp.where(here, cols[:, 2:3], 0.0).astype(bf16),
                ],
                axis=1,
            )
            rows = dot(place, jnp.concatenate([x, x], axis=0)).astype(bf16)
            rows_ref[:, q * PCAP : (q + 1) * PCAP, :] = rows.reshape(EY // 2, PCAP, DZ)
            q += 1
    for i in range(NZ // 2):
        label_ref[i] = labels[i * EO : (i + 1) * EO]


def back_kernel(at_ref, own_ref, mine_ref, other_ref, out_ref, up_ref, table_ref):
    me_y, me_x, me_core = at_ref[0], at_ref[1], at_ref[2]
    token = (iota((TOK, 256), 0) + 1).astype(f32)
    group = iota((R, 256), 1) >> 4
    first = iota((R, 128), 1) < 64
    for k in range(NY):
        g = ((me_x + RING[k]) & 3) * 2
        up_ref[g + me_core] = mine_ref[k]
        up_ref[g + 1 - me_core] = other_ref[k]
    for q in range(NZ):
        table_ref[q] = own_ref[q, TOK:MROWS, :].astype(f32)

    def pair(p, carry):
        x = jnp.concatenate([own_ref[2 * p, 0:TOK, :], own_ref[2 * p + 1, 0:TOK, :]], axis=0)
        at = pl.multiple_of(p * R, R)
        for k in range(NY):
            y = (me_y + RING[k]) & 3
            up = jnp.concatenate([up_ref[g, k] for g in range(DP)], axis=0)
            dense = dot(up, x, 1, 1)
            dense = jnp.concatenate(
                [dense[g * 64 + zo * 8 : g * 64 + zo * 8 + 8] for zo in range(NZ) for g in range(DP)],
                axis=0,
            )
            high = dense.astype(bf16)
            low = (dense - high.astype(f32)).astype(bf16)
            for c in range(2):
                found = []
                for h in range(2):
                    def entry(kind):
                        return table_ref[2 * p + h, pl.ds(4 * kind + y, 1), c * 256 : (c + 1) * 256]

                    place = jnp.where(entry(0) == token, 1.0, 0.0).astype(bf16)
                    part = dot(
                        jnp.concatenate(
                            [
                                v[c * 256 : (c + 1) * 256, h * TOK : (h + 1) * TOK]
                                for v in (high, low)
                            ],
                            axis=1,
                        ),
                        jnp.concatenate([place, place], axis=0),
                    )
                    total = jnp.where(group == 0, part[0:R], 0.0)
                    for e in range(1, 16):
                        total = jnp.where(group == e, part[e * R : (e + 1) * R], total)
                    found.append(total * (entry(1) + entry(2)))
                for t in range(2):
                    a, b = (v[:, t * 128 : (t + 1) * 128] for v in found)
                    o = y * NZ + c * 4 + t * 2
                    out_ref[o, pl.ds(at, R), :] = jnp.where(first, a, pltpu.roll(b, 64, 1)).astype(bf16)
                    out_ref[o + 1, pl.ds(at, R), :] = jnp.where(first, pltpu.roll(a, 64, 1), b).astype(bf16)
        return carry

    lax.fori_loop(0, NZ // 2, pair, 0, unroll=True)

    half = iota((NZ, 128), 1) < 64
    pad = jnp.zeros((8, 128), f32)
    for y in range(NY):
        def label(h):
            rows = [table_ref[2 * p + h, 12 + y : 13 + y, :] for p in range(NZ // 2)]
            return jnp.concatenate(rows + [jnp.zeros((4, DZ), f32)], axis=0)

        even, odd = label(0), label(1)
        for t in range(4):
            a, b = even[:, t * 128 : (t + 1) * 128], odd[:, t * 128 : (t + 1) * 128]
            o = y * NZ + t * 2
            for i, v in enumerate(
                (jnp.where(half, a, pltpu.roll(b, 64, 1)), jnp.where(half, pltpu.roll(a, 64, 1), b))
            ):
                out_ref[o + i, EO * R : EO * R + 16, :] = jnp.concatenate([v, pad], axis=0).astype(bf16)


def squares(v):
    v = v * v
    total = v[:, 0:128]
    for c in range(1, v.shape[1] // 128):
        total = total + v[:, c * 128 : (c + 1) * 128]
    return total


def spread(label, value):
    label = jnp.broadcast_to(label, value.shape).astype(bf16)
    value = value.astype(bf16)
    return jnp.concatenate(
        [jnp.where(label == n + 1.0, value, jnp.zeros_like(value)) for n in range(NEX)], axis=0
    )


def b_kernel(y_ref, own, right, far, left, lab0, lab1, lab2, lab3, *refs):
    low_refs, (sqa_ref, out_ref, norm_ref, sq_ref, low_ref) = refs[:3], refs[3:]
    i = pl.program_id(0)
    y = y_ref[0]

    @pl.when(i == 0)
    def _():
        sq_ref[...] = sqa_ref[...]
        for ref, places in zip(low_refs, LOWS):
            for n, k in enumerate(places):
                low_ref[(y_ref[3] + k) & (NZ - 1)] = ref[n * EO * R : (n + 1) * EO * R, :]

    total = jnp.zeros((NEX * R, 128), f32)
    for j in range(EO):
        label = jnp.concatenate([v[0, j : j + 1, :] for v in (lab0, lab1, lab2, lab3)], axis=1)
        low = jnp.concatenate(
            [
                low_ref[i, j * R : (j + 1) * R, pl.ds(pl.multiple_of(((y + k) & 3) * 128, 128), 128)]
                for k in range(NY)
            ],
            axis=1,
        )
        rows = jnp.concatenate([own[j], right[j], far[j], left[j]], axis=0)
        b = dot(spread(label, low), rows)
        total = total + squares(b)
        out_ref[j] = b.astype(bf16)
    sq_ref[...] += total

    @pl.when(i == NZ - 1)
    def _():
        s = jnp.sum(sq_ref[...].reshape(NEX, R, 128), axis=1)
        s = jnp.broadcast_to(jnp.sum(s, axis=1, keepdims=True), (NEX, 128)) * (SCALE * SCALE)
        s = jnp.where(iota((NEX, 128), 1) >> 3 == iota((NEX, 128), 0), s, 0.0)
        norm_ref[...] = jnp.broadcast_to(jnp.sum(s, axis=0, keepdims=True), norm_ref.shape)


def a_kernel(back_ref, hidden_ref, slots_ref, a_ref, sq_ref, total_ref):
    j = pl.program_id(0)

    @pl.when(j == 0)
    def _():
        sq_ref[...] = jnp.zeros_like(sq_ref)
        for k in range(NY):
            total = back_ref[k * NZ, 0 : EO * R, :].astype(f32)
            for z in range(1, NZ):
                total = total + back_ref[k * NZ + z, 0 : EO * R, :].astype(f32)
            labels = back_ref[k * NZ, EO * R : BROWS, :].astype(f32)
            for p in range(NZ // 2):
                at = (k * 4 + p) * 128
                total_ref[0:R, at : at + 128] = total[p * R : (p + 1) * R].astype(bf16)
                total_ref[R : 2 * R, at : at + 128] = jnp.broadcast_to(
                    labels[p : p + 1], (R, 128)
                ).astype(bf16)

    tiles = []
    for c in range(3):
        lane = iota((768, 128), 0) + c * 640
        s = lane & (PCAP - 1)
        at = jnp.where(((lane >> 4) & 3 == j) & (s < CAP), (lane >> 6) * CAP + s, -1)
        pick = jnp.where(at == iota((768, 128), 1) + c * 128, 1.0, 0.0).astype(bf16)
        tiles.append(dot(total_ref[:, c * 640 : c * 640 + 768], pick))
    tiles = jnp.concatenate(tiles, axis=1)
    back, label = tiles[0:R], tiles[R : R + 1]
    a = dot(spread(label, back), hidden_ref[0])
    sq_ref[...] += squares(a)
    a_ref[0] = a.astype(bf16)
    slots_ref[0] = back.astype(bf16)


def hidden_kernel(slots_ref, down_ref, grad_ref):
    grad_ref[0] = (SCALE * dot(slots_ref[0], down_ref[0], 0, 0)).astype(bf16)


def clip_kernel(norm_ref, b_ref, a_ref, out_ref, ga_ref):
    i = pl.program_id(0)
    radius = math.sqrt(EXP * R * (D + F) / (DP * NEX))
    norm = jnp.sum(norm_ref[...], axis=0, keepdims=True)
    norm = jnp.where(iota((NEX, 128), 1) == iota((NEX, 128), 0) * 8, norm, 0.0)
    norm = jnp.broadcast_to(jnp.sum(norm, axis=1, keepdims=True), (NEX, 128))
    factor = SCALE * radius / (jnp.sqrt(norm) + GAMMA)
    wide = jnp.concatenate([factor, factor], axis=1)
    column = iota((NEX, NEX * R), 1)
    wide = jnp.sum(jnp.where(column >> 4 == iota((NEX, NEX * R), 0), wide, 0.0), axis=0, keepdims=True)
    wide = jnp.where(column & 15 == iota((R, NEX * R), 0), wide, 0.0)
    high = wide.astype(bf16)
    pick = jnp.concatenate([high, (wide - high.astype(f32)).astype(bf16)], axis=0)

    def weighted(v):
        v = dot(pick, v)
        return v[0:R] + v[R:]

    @pl.when(i == 0)
    def _():
        for j in range(EO):
            ga_ref[j * R : (j + 1) * R, :] = weighted(a_ref[j])
        for d in range(DP):
            out_ref[d, :, DZ : DZ + FA] = ga_ref[:, d * FA : (d + 1) * FA].astype(bf16)

    for j in range(EO):
        out_ref[i, j * R : (j + 1) * R, 0:DZ] = weighted(b_ref[j]).astype(bf16)


def shape(*dims, dtype=bf16):
    return jax.ShapeDtypeStruct(dims, dtype)


def whole(*dims):
    return pl.BlockSpec(dims, lambda i: (0,) * len(dims))


def call(kernel, name, cost=1, **kw):
    return pl.pallas_call(
        kernel,
        name=name,
        compiler_params=pltpu.CompilerParams(**PARAMS),
        cost_estimate=pl.CostEstimate(flops=max(cost << 30, 1024), bytes_accessed=1024, transcendentals=0),
        **kw,
    )


def in_hbm(v):
    return pltpu.with_memory_space_constraint(v, pltpu.HBM)


def shards(grad, gates, routes, example, hidden, down, up):
    me = lax.axis_index("expert")
    group = lax.axis_index("dp")
    here = jnp.stack([me // NZ, group // 2, group % 2, me % NZ]).astype(i32)
    hidden = in_hbm(hidden[0])

    def over_y(v, k):
        pairs = [(a * NZ + b, ((a + k) % NY) * NZ + b) for a in range(NY) for b in range(NZ)]
        return lax.ppermute(v, "expert", pairs)

    def over_x(v, k):
        pairs = [(a * 2 + b, ((a + k) % 4) * 2 + b) for a in range(4) for b in range(2)]
        return lax.ppermute(v, "dp", pairs)

    def ring(v, over, *beside):
        left, right = over(v, 1), over(v, 3)
        if beside:
            left, right, *beside = lax.optimization_barrier((left, right, *beside))
        half = v.shape[0] // 2
        return [*beside, jnp.concatenate([v, left, right, over(left[:half], 1), over(right[half:], 3)])]

    part = lax.dynamic_slice_in_dim(up.reshape(EO * R, D), group * 8, 8, 0)
    part = part.reshape(8, NZ, DZ).transpose(1, 0, 2)
    part = lax.all_to_all(part, "expert", 0, 0, axis_index_groups=ZGROUPS, tiled=True)
    m1 = call(
        send_kernel, "send",
        grid=(1,),
        in_specs=[whole(TOK, D), whole(TOPK, TOK), whole(TOPK, TOK), whole(1, TOK)],
        out_specs=whole(NZ, MROWS, DZ), out_shape=shape(NZ, MROWS, DZ),
    )(*[in_hbm(v) for v in (grad[0], gates[0].T, routes[0].T, example)])

    m1, down_low = lax.optimization_barrier((m1, down))
    own = lax.all_to_all(m1, "expert", 0, 0, axis_index_groups=ZGROUPS, tiled=True)
    low = call(
        low_kernel, "low",
        grid=(EO,),
        in_specs=[
            pl.BlockSpec((1, SLOTS, F), lambda i: (i, 0, 0)),
            pl.BlockSpec((1, R, F), lambda i: (i, 0, 0)),
        ],
        out_specs=pl.BlockSpec((R, PSLOTS), lambda i: (i, 0)),
        out_shape=shape(EO * R, PSLOTS),
    )(hidden, down_low)
    low, mine = ring(*ring(part.reshape(NZ * 8, DZ), over_y), over_x, low)

    def over_z(v, k):
        pairs = [(a * NZ + b, a * NZ + (b + k) % NZ) for a in range(NY) for b in range(NZ)]
        return lax.ppermute(v, "expert", pairs)

    near0, near1 = over_z(low, 1), over_z(low, NZ - 1)
    near0, near1, mine = lax.optimization_barrier((near0, near1, mine))
    lows = [jnp.concatenate([low, near0, near1]), jnp.concatenate([low, near0])]
    other = lax.ppermute(mine, "dp", [(g, g ^ 1) for g in range(DP)])
    mine, other = (v.reshape(4, NY, NZ * 8, DZ) for v in (mine, other))

    low_half, high_half = own[: NZ // 2], own[NZ // 2 :]
    left0, right1 = over_y(low_half, 1), over_y(high_half, NY - 1)
    left1, right0 = over_y(high_half, 1), over_y(low_half, NY - 1)

    def gather(cost, *blocks, space=pltpu.HBM):
        return call(
            gather_kernel, "gather", cost,
            grid=(2,),
            in_specs=[SMEM] + [whole(*v.shape) for v in blocks],
            out_specs=[
                pl.BlockSpec((EY // 2, NZ * PCAP, DZ), lambda i: (i, 0, 0)),
                pl.BlockSpec((NZ // 2, EO, NZ * PCAP), lambda i: (i, 0, 0)),
            ],
            out_shape=[space((EY, NZ * PCAP, DZ), bf16), shape(NZ, EO, NZ * PCAP, dtype=f32)],
        )(here, *blocks)

    sent = call(
        back_kernel, "back", 60,
        in_specs=[SMEM] + [VMEM] * 3, out_specs=VMEM, out_shape=shape(NSRC, BROWS, 128),
        scratch_shapes=[
            pltpu.VMEM((DP, NY, NZ * 8, DZ), bf16),
            pltpu.VMEM((NZ, 16, DZ), f32),
        ],
    )(here, own, mine, other)
    back = lax.all_to_all(sent, "expert", 0, 0, tiled=True)

    own, sent = lax.optimization_barrier((own, sent))

    def over_z(v, k):
        pairs = [(a * NZ + b, a * NZ + (b + k) % NZ) for a in range(NY) for b in range(NZ)]
        return lax.ppermute(v, "expert", pairs)

    part_own = gather(0, own)
    left0, right0, right1, part_own, *lows = lax.optimization_barrier(
        (left0, right0, right1, part_own, *lows)
    )
    far0, far1 = over_y(left0, 1), over_y(right1, NY - 1)
    lows = [lows[0], over_z(lows[0], 3), over_z(lows[1], NZ - 3)]
    part_right = gather(80, right0, right1)
    left1, part_right = lax.optimization_barrier((left1, part_right))
    part_left = gather(0, left0, left1)
    back, part_right, part_left = lax.optimization_barrier((back, part_right, part_left))
    slots, big_a, sq_a = call(
        a_kernel, "norm_a", 0,
        grid=(EO,),
        in_specs=[
            whole(NSRC, BROWS, 128),
            pl.BlockSpec((1, SLOTS, F), lambda i: (i, 0, 0)),
        ],
        out_specs=[
            pl.BlockSpec((1, R, SLOTS), lambda i: (i, 0, 0)),
            pl.BlockSpec((1, NEX * R, F), lambda i: (i, 0, 0)),
            whole(NEX * R, 128),
        ],
        out_shape=[
            shape(EO, R, SLOTS),
            shape(EO, NEX * R, F),
            shape(NEX * R, 128, dtype=f32),
        ],
        scratch_shapes=[pltpu.VMEM((2 * R, NSRC * 64), bf16)],
    )(back, hidden)

    far0, far1, sq_a = lax.optimization_barrier((far0, far1, sq_a))
    parts = [part_own, part_right, gather(0, far0, far1, space=pltpu.VMEM), part_left]
    big_b, norm = call(
        b_kernel, "norm_b",
        grid=(NZ,),
        in_specs=[SMEM]
        + [pl.BlockSpec((EO, NZ * PCAP, DZ), lambda i: (i, 0, 0))] * 4
        + [pl.BlockSpec((1, EO, NZ * PCAP), lambda i: (i, 0, 0))] * 4
        + [
            *[whole(len(v) * EO * R, PSLOTS) for v in LOWS],
            whole(NEX * R, 128),
        ],
        out_specs=[
            pl.BlockSpec((EO, NEX * R, DZ), lambda i: (i, 0, 0)),
            whole(NSRC, 128),
        ],
        out_shape=[shape(EY, NEX * R, DZ), shape(NSRC, 128, dtype=f32)],
        scratch_shapes=[
            pltpu.VMEM((NEX * R, 128), f32),
            pltpu.VMEM((NZ, EO * R, PSLOTS), bf16),
        ],
    )(here, *[
            pltpu.with_memory_space_constraint(v[0], pltpu.VMEM if n == 2 else pltpu.HBM)
            for n, v in enumerate(parts)
        ], *[v[1] for v in parts], *lows, sq_a)
    norm = lax.all_to_all(norm, "expert", 0, 0, tiled=True)

    sums = call(
        clip_kernel, "clip",
        grid=(NZ,),
        in_specs=[
            whole(NSRC, 128),
            pl.BlockSpec((EO, NEX * R, DZ), lambda i: (i, 0, 0)),
            whole(EO, NEX * R, F),
        ],
        out_specs=whole(DP, EO * R, DZ + FA),
        out_shape=shape(DP, EO * R, DZ + FA),
        scratch_shapes=[pltpu.VMEM((EO * R, F), f32)],
    )(norm, big_b, big_a)
    slots, sums = lax.optimization_barrier((slots, sums))
    sums = lax.all_to_all(sums, "dp", 0, 0, tiled=True)
    hidden_grad = call(
        hidden_kernel, "hidden_grad",
        grid=(EO,),
        in_specs=[
            pl.BlockSpec((1, R, SLOTS), lambda i: (i, 0, 0)),
            pl.BlockSpec((1, R, F), lambda i: (i, 0, 0)),
        ],
        out_specs=pl.BlockSpec((1, SLOTS, F), lambda i: (i, 0, 0)),
        out_shape=shape(EO, SLOTS, F),
    )(slots, down)
    sums, hidden_grad = lax.optimization_barrier((sums, hidden_grad))
    sums = jnp.sum(sums.astype(f32), axis=0)
    swap = [
        ((g * NY + a) * NZ + b, (b * NY + a) * NZ + g)
        for g in range(DP) for a in range(NY) for b in range(NZ)
    ]
    grad_b = lax.ppermute(sums[:, :DZ].astype(bf16), ("dp", "expert"), swap).astype(f32)
    return (
        hidden_grad[None],
        sums[:, DZ:].reshape(EO, R, FA),
        grad_b.reshape(EO, R, DZ),
    )


def solution(mesh):
    return jax.shard_map(
        shards,
        mesh=mesh,
        in_specs=(
            P("dp", "expert", None),
            P("dp", "expert", None),
            P("dp", "expert", None),
            P("dp", "expert"),
            P("dp", "expert", None, None),
            P("expert", None, None),
            P("expert", None, None),
        ),
        out_specs=(P("dp", "expert", None, None), P("expert", None, "dp"), P("expert", None, "dp")),
        check_vma=False,
    )
```

```python
import math

import jax
import jax.numpy as jnp
from jax import lax
from jax.experimental import pallas as pl
from jax.experimental.pallas import tpu as pltpu
from jax.sharding import PartitionSpec as P

NY, NZ, DP = 4, 8, 8
NSRC = NY * NZ
TOK = 128
TOPK = 8
D = 4096
DZ = D // NZ
F = 1536
R = 16
EXP = 128
EO = 4
EY = EXP // NY
CAP = 12
PCAP = 16
SLOTS = NSRC * CAP
PSLOTS = NSRC * PCAP
NEX = 16
MROWS = TOK + 16
SCALE = 2.0
GAMMA = 0.01
FA = F // DP
f32 = jnp.float32
bf16 = jnp.bfloat16
i32 = jnp.int32

ZGROUPS = [[y * NZ + z for z in range(NZ)] for y in range(NY)]
RING = (0, 3, 1, 2)
LOWS = ((0, -1, 1), (-3, -4, -2), (3, 2))
HALF = EY * PCAP // 2
BROWS = EO * R + 16
VMEM = pl.BlockSpec(memory_space=pltpu.VMEM)
SMEM = pl.BlockSpec(memory_space=pltpu.SMEM)
PARAMS = dict(vmem_limit_bytes=14 * 1024 * 1024)


def dot(a, b, ca=1, cb=0):
    return lax.dot_general(a, b, (((ca,), (cb,)), ((), ())), preferred_element_type=f32)


def iota(shape, dim):
    return lax.broadcasted_iota(i32, shape, dim)


def pad_matrix():
    lane = iota((SLOTS, PSLOTS), 1)
    s = lane & (PCAP - 1)
    at = (lane >> 4) * CAP + s
    return jnp.where((at == iota((SLOTS, PSLOTS), 0)) & (s < CAP), 1.0, 0.0).astype(bf16)


def send_kernel(x_ref, gate_ref, route_ref, example_ref, out_ref):
    gate_of = gate_ref[...].T
    route_of = route_ref[...].astype(f32).T.astype(i32)
    expert = iota((TOK, EXP), 1)
    routed = jnp.zeros((TOK, EXP), f32)
    gate = jnp.zeros((TOK, EXP), f32)
    for k in range(TOPK):
        hit = route_of[:, k : k + 1] == expert
        routed = jnp.where(hit, 1.0, routed)
        gate = jnp.where(hit, gate_of[:, k : k + 1], gate)
    before = jnp.where(iota((TOK, TOK), 1) < iota((TOK, TOK), 0), 1.0, 0.0).astype(bf16)
    rank = jnp.where(routed > 0.5, dot(before, routed.astype(bf16)), 64.0).astype(bf16)
    high = gate.astype(bf16)
    low = (gate - high.astype(f32)).astype(bf16)
    row = iota((16, TOK), 0)
    ids = jnp.where(
        row == 0,
        iota((16, TOK), 1) + 1,
        jnp.where(row == 1, jnp.broadcast_to(example_ref[...], (16, TOK)) + 1, 0),
    ).astype(f32).astype(bf16)
    ones = jnp.ones((16, TOK), bf16)
    toks, highs, lows, labels = [], [], [], []
    for y in range(NY):
        lane = iota((EXP, EY * PCAP), 1)
        expand = jnp.where((lane >> 4) + y * EY == iota((EXP, EY * PCAP), 0), 1.0, 0.0).astype(bf16)
        place = (iota((TOK, EY * PCAP), 1) & (PCAP - 1)).astype(f32)
        here = dot(rank, expand) == place
        tab = dot(ids, jnp.where(here, 1.0, 0.0).astype(bf16))
        toks.append(tab[0:1])
        labels.append(tab[1:2])
        highs.append(dot(ones, jnp.where(here, dot(high, expand), 0.0).astype(bf16))[0:1])
        lows.append(dot(ones, jnp.where(here, dot(low, expand), 0.0).astype(bf16))[0:1])
    table = jnp.concatenate(toks + highs + lows + labels, axis=0).astype(bf16)
    for z in range(NZ):
        out_ref[z, 0:TOK, :] = x_ref[:, z * DZ : (z + 1) * DZ]
        out_ref[z, TOK:MROWS, :] = table


def low_kernel(hidden_ref, down_ref, out_ref):
    low = dot(down_ref[0], hidden_ref[0], 1, 1).astype(bf16)
    low = dot(low, pad_matrix()).astype(bf16)
    out_ref[...] = low


def gather_kernel(y_ref, *refs):
    blocks, (rows_ref, label_ref) = refs[:-2], refs[-2:]
    y = y_ref[0]
    lanes = pl.ds(pl.multiple_of(pl.program_id(0) * HALF, HALF), HALF)
    row = iota((16, HALF), 0)
    token = iota((HALF, TOK), 1) + 1
    lane = iota((EY // 2, HALF), 1)
    expert = iota((EY // 2, HALF), 0)
    labels = jnp.zeros((EY // 2, NZ * PCAP), f32)
    q = 0
    for block_ref in blocks:
        for i in range(block_ref.shape[0]):
            x = block_ref[i, 0:TOK, :]
            table = block_ref[i, TOK:MROWS, lanes].astype(f32)

            def pick(k):
                return jnp.sum(jnp.where(row == 4 * k + y, table, 0.0), axis=0, keepdims=True)

            tok, high, low, label = pick(0), pick(1), pick(2), pick(3)
            here = jnp.where(lane >> 4 == expert, label, 0.0).astype(bf16)
            at = (iota((HALF, NZ * PCAP), 0) & (PCAP - 1)) + q * PCAP
            move = jnp.where(at == iota((HALF, NZ * PCAP), 1), 1.0, 0.0).astype(bf16)
            labels = labels + dot(here, move)
            cols = jnp.concatenate([tok, high, low, jnp.zeros((5, HALF), f32)], axis=0).T
            here = cols[:, 0:1].astype(i32) == token
            place = jnp.concatenate(
                [
                    jnp.where(here, cols[:, 1:2], 0.0).astype(bf16),
                    jnp.where(here, cols[:, 2:3], 0.0).astype(bf16),
                ],
                axis=1,
            )
            rows = dot(place, jnp.concatenate([x, x], axis=0)).astype(bf16)
            rows_ref[:, q * PCAP : (q + 1) * PCAP, :] = rows.reshape(EY // 2, PCAP, DZ)
            q += 1
    for i in range(NZ // 2):
        label_ref[i] = labels[i * EO : (i + 1) * EO]


def back_kernel(at_ref, own_ref, mine_ref, other_ref, out_ref, up_ref, table_ref):
    me_y, me_x, me_core = at_ref[0], at_ref[1], at_ref[2]
    token = (iota((TOK, 256), 0) + 1).astype(f32)
    group = iota((R, 256), 1) >> 4
    first = iota((R, 128), 1) < 64
    for k in range(NY):
        g = ((me_x + RING[k]) & 3) * 2
        up_ref[g + me_core] = mine_ref[k]
        up_ref[g + 1 - me_core] = other_ref[k]
    for q in range(NZ):
        table_ref[q] = own_ref[q, TOK:MROWS, :].astype(f32)

    def pair(p, carry):
        x = jnp.concatenate([own_ref[2 * p, 0:TOK, :], own_ref[2 * p + 1, 0:TOK, :]], axis=0)
        at = pl.multiple_of(p * R, R)
        for k in range(NY):
            y = (me_y + RING[k]) & 3
            up = jnp.concatenate([up_ref[g, k] for g in range(DP)], axis=0)
            dense = dot(up, x, 1, 1)
            dense = jnp.concatenate(
                [dense[g * 64 + zo * 8 : g * 64 + zo * 8 + 8] for zo in range(NZ) for g in range(DP)],
                axis=0,
            )
            high = dense.astype(bf16)
            low = (dense - high.astype(f32)).astype(bf16)
            for c in range(2):
                found = []
                for h in range(2):
                    def entry(kind):
                        return table_ref[2 * p + h, pl.ds(4 * kind + y, 1), c * 256 : (c + 1) * 256]

                    place = jnp.where(entry(0) == token, 1.0, 0.0).astype(bf16)
                    part = dot(
                        jnp.concatenate(
                            [
                                v[c * 256 : (c + 1) * 256, h * TOK : (h + 1) * TOK]
                                for v in (high, low)
                            ],
                            axis=1,
                        ),
                        jnp.concatenate([place, place], axis=0),
                    )
                    total = jnp.where(group == 0, part[0:R], 0.0)
                    for e in range(1, 16):
                        total = jnp.where(group == e, part[e * R : (e + 1) * R], total)
                    found.append(total * (entry(1) + entry(2)))
                for t in range(2):
                    a, b = (v[:, t * 128 : (t + 1) * 128] for v in found)
                    o = y * NZ + c * 4 + t * 2
                    out_ref[o, pl.ds(at, R), :] = jnp.where(first, a, pltpu.roll(b, 64, 1)).astype(bf16)
                    out_ref[o + 1, pl.ds(at, R), :] = jnp.where(first, pltpu.roll(a, 64, 1), b).astype(bf16)
        return carry

    lax.fori_loop(0, NZ // 2, pair, 0, unroll=True)

    half = iota((NZ, 128), 1) < 64
    pad = jnp.zeros((8, 128), f32)
    for y in range(NY):
        def label(h):
            rows = [table_ref[2 * p + h, 12 + y : 13 + y, :] for p in range(NZ // 2)]
            return jnp.concatenate(rows + [jnp.zeros((4, DZ), f32)], axis=0)

        even, odd = label(0), label(1)
        for t in range(4):
            a, b = even[:, t * 128 : (t + 1) * 128], odd[:, t * 128 : (t + 1) * 128]
            o = y * NZ + t * 2
            for i, v in enumerate(
                (jnp.where(half, a, pltpu.roll(b, 64, 1)), jnp.where(half, pltpu.roll(a, 64, 1), b))
            ):
                out_ref[o + i, EO * R : EO * R + 16, :] = jnp.concatenate([v, pad], axis=0).astype(bf16)


def squares(v):
    v = v * v
    total = v[:, 0:128]
    for c in range(1, v.shape[1] // 128):
        total = total + v[:, c * 128 : (c + 1) * 128]
    return total


def spread(label, value):
    label = jnp.broadcast_to(label, value.shape).astype(bf16)
    value = value.astype(bf16)
    return jnp.concatenate(
        [jnp.where(label == n + 1.0, value, jnp.zeros_like(value)) for n in range(NEX)], axis=0
    )


def b_kernel(y_ref, own, right, far, left, lab0, lab1, lab2, lab3, *refs):
    low_refs, (sqa_ref, out_ref, norm_ref, sq_ref, low_ref) = refs[:3], refs[3:]
    i = pl.program_id(0)
    y = y_ref[0]

    @pl.when(i == 0)
    def _():
        sq_ref[...] = sqa_ref[...]
        for ref, places in zip(low_refs, LOWS):
            for n, k in enumerate(places):
                low_ref[(y_ref[3] + k) & (NZ - 1)] = ref[n * EO * R : (n + 1) * EO * R, :]

    total = jnp.zeros((NEX * R, 128), f32)
    for j in range(EO):
        label = jnp.concatenate([v[0, j : j + 1, :] for v in (lab0, lab1, lab2, lab3)], axis=1)
        low = jnp.concatenate(
            [
                low_ref[i, j * R : (j + 1) * R, pl.ds(pl.multiple_of(((y + k) & 3) * 128, 128), 128)]
                for k in range(NY)
            ],
            axis=1,
        )
        rows = jnp.concatenate([own[j], right[j], far[j], left[j]], axis=0)
        b = dot(spread(label, low), rows)
        total = total + squares(b)
        out_ref[j] = b.astype(bf16)
    sq_ref[...] += total

    @pl.when(i == NZ - 1)
    def _():
        s = jnp.sum(sq_ref[...].reshape(NEX, R, 128), axis=1)
        s = jnp.broadcast_to(jnp.sum(s, axis=1, keepdims=True), (NEX, 128)) * (SCALE * SCALE)
        s = jnp.where(iota((NEX, 128), 1) >> 3 == iota((NEX, 128), 0), s, 0.0)
        norm_ref[...] = jnp.broadcast_to(jnp.sum(s, axis=0, keepdims=True), norm_ref.shape)


def a_kernel(back_ref, hidden_ref, slots_ref, a_ref, sq_ref, total_ref):
    j = pl.program_id(0)

    @pl.when(j == 0)
    def _():
        sq_ref[...] = jnp.zeros_like(sq_ref)
        for k in range(NY):
            total = back_ref[k * NZ, 0 : EO * R, :].astype(f32)
            for z in range(1, NZ):
                total = total + back_ref[k * NZ + z, 0 : EO * R, :].astype(f32)
            labels = back_ref[k * NZ, EO * R : BROWS, :].astype(f32)
            for p in range(NZ // 2):
                at = (k * 4 + p) * 128
                total_ref[0:R, at : at + 128] = total[p * R : (p + 1) * R].astype(bf16)
                total_ref[R : 2 * R, at : at + 128] = jnp.broadcast_to(
                    labels[p : p + 1], (R, 128)
                ).astype(bf16)

    tiles = []
    for c in range(3):
        lane = iota((768, 128), 0) + c * 640
        s = lane & (PCAP - 1)
        at = jnp.where(((lane >> 4) & 3 == j) & (s < CAP), (lane >> 6) * CAP + s, -1)
        pick = jnp.where(at == iota((768, 128), 1) + c * 128, 1.0, 0.0).astype(bf16)
        tiles.append(dot(total_ref[:, c * 640 : c * 640 + 768], pick))
    tiles = jnp.concatenate(tiles, axis=1)
    back, label = tiles[0:R], tiles[R : R + 1]
    a = dot(spread(label, back), hidden_ref[0])
    sq_ref[...] += squares(a)
    a_ref[0] = a.astype(bf16)
    slots_ref[0] = back.astype(bf16)


def hidden_kernel(slots_ref, down_ref, grad_ref):
    grad_ref[0] = (SCALE * dot(slots_ref[0], down_ref[0], 0, 0)).astype(bf16)


def clip_kernel(norm_ref, b_ref, a_ref, out_ref, ga_ref):
    i = pl.program_id(0)
    radius = math.sqrt(EXP * R * (D + F) / (DP * NEX))
    norm = jnp.sum(norm_ref[...], axis=0, keepdims=True)
    norm = jnp.where(iota((NEX, 128), 1) == iota((NEX, 128), 0) * 8, norm, 0.0)
    norm = jnp.broadcast_to(jnp.sum(norm, axis=1, keepdims=True), (NEX, 128))
    factor = SCALE * radius / (jnp.sqrt(norm) + GAMMA)
    wide = jnp.concatenate([factor, factor], axis=1)
    column = iota((NEX, NEX * R), 1)
    wide = jnp.sum(jnp.where(column >> 4 == iota((NEX, NEX * R), 0), wide, 0.0), axis=0, keepdims=True)
    wide = jnp.where(column & 15 == iota((R, NEX * R), 0), wide, 0.0)
    high = wide.astype(bf16)
    pick = jnp.concatenate([high, (wide - high.astype(f32)).astype(bf16)], axis=0)

    def weighted(v):
        v = dot(pick, v)
        return v[0:R] + v[R:]

    @pl.when(i == 0)
    def _():
        for j in range(EO):
            ga_ref[j * R : (j + 1) * R, :] = weighted(a_ref[j])
        for d in range(DP):
            out_ref[d, :, DZ : DZ + FA] = ga_ref[:, d * FA : (d + 1) * FA].astype(bf16)

    for j in range(EO):
        out_ref[i, j * R : (j + 1) * R, 0:DZ] = weighted(b_ref[j]).astype(bf16)


def shape(*dims, dtype=bf16):
    return jax.ShapeDtypeStruct(dims, dtype)


def whole(*dims):
    return pl.BlockSpec(dims, lambda i: (0,) * len(dims))


def call(kernel, name, cost=1, **kw):
    return pl.pallas_call(
        kernel,
        name=name,
        compiler_params=pltpu.CompilerParams(**PARAMS),
        cost_estimate=pl.CostEstimate(flops=max(cost << 30, 1024), bytes_accessed=1024, transcendentals=0),
        **kw,
    )


def in_hbm(v):
    return pltpu.with_memory_space_constraint(v, pltpu.HBM)


def shards(grad, gates, routes, example, hidden, down, up):
    me = lax.axis_index("expert")
    group = lax.axis_index("dp")
    here = jnp.stack([me // NZ, group // 2, group % 2, me % NZ]).astype(i32)
    hidden = in_hbm(hidden[0])

    def over_y(v, k):
        pairs = [(a * NZ + b, ((a + k) % NY) * NZ + b) for a in range(NY) for b in range(NZ)]
        return lax.ppermute(v, "expert", pairs)

    def over_x(v, k):
        pairs = [(a * 2 + b, ((a + k) % 4) * 2 + b) for a in range(4) for b in range(2)]
        return lax.ppermute(v, "dp", pairs)

    def ring(v, over, *beside):
        left, right = over(v, 1), over(v, 3)
        if beside:
            left, right, *beside = lax.optimization_barrier((left, right, *beside))
        half = v.shape[0] // 2
        return [*beside, jnp.concatenate([v, left, right, over(left[:half], 1), over(right[half:], 3)])]

    part = lax.dynamic_slice_in_dim(up.reshape(EO * R, D), group * 8, 8, 0)
    part = part.reshape(8, NZ, DZ).transpose(1, 0, 2)
    part = lax.all_to_all(part, "expert", 0, 0, axis_index_groups=ZGROUPS, tiled=True)
    m1 = call(
        send_kernel, "send",
        grid=(1,),
        in_specs=[whole(TOK, D), whole(TOPK, TOK), whole(TOPK, TOK), whole(1, TOK)],
        out_specs=whole(NZ, MROWS, DZ), out_shape=shape(NZ, MROWS, DZ),
    )(*[in_hbm(v) for v in (grad[0], gates[0].T, routes[0].T, example)])

    m1, down_low = lax.optimization_barrier((m1, down))
    own = lax.all_to_all(m1, "expert", 0, 0, axis_index_groups=ZGROUPS, tiled=True)
    low = call(
        low_kernel, "low",
        grid=(EO,),
        in_specs=[
            pl.BlockSpec((1, SLOTS, F), lambda i: (i, 0, 0)),
            pl.BlockSpec((1, R, F), lambda i: (i, 0, 0)),
        ],
        out_specs=pl.BlockSpec((R, PSLOTS), lambda i: (i, 0)),
        out_shape=shape(EO * R, PSLOTS),
    )(hidden, down_low)
    low, mine = ring(*ring(part.reshape(NZ * 8, DZ), over_y), over_x, low)

    def over_z(v, k):
        pairs = [(a * NZ + b, a * NZ + (b + k) % NZ) for a in range(NY) for b in range(NZ)]
        return lax.ppermute(v, "expert", pairs)

    near0, near1 = over_z(low, 1), over_z(low, NZ - 1)
    near0, near1, mine = lax.optimization_barrier((near0, near1, mine))
    lows = [jnp.concatenate([low, near0, near1]), jnp.concatenate([low, near0])]
    other = lax.ppermute(mine, "dp", [(g, g ^ 1) for g in range(DP)])
    mine, other = (v.reshape(4, NY, NZ * 8, DZ) for v in (mine, other))

    low_half, high_half = own[: NZ // 2], own[NZ // 2 :]
    left0, right1 = over_y(low_half, 1), over_y(high_half, NY - 1)
    left1, right0 = over_y(high_half, 1), over_y(low_half, NY - 1)

    def gather(cost, *blocks, space=pltpu.HBM):
        return call(
            gather_kernel, "gather", cost,
            grid=(2,),
            in_specs=[SMEM] + [whole(*v.shape) for v in blocks],
            out_specs=[
                pl.BlockSpec((EY // 2, NZ * PCAP, DZ), lambda i: (i, 0, 0)),
                pl.BlockSpec((NZ // 2, EO, NZ * PCAP), lambda i: (i, 0, 0)),
            ],
            out_shape=[space((EY, NZ * PCAP, DZ), bf16), shape(NZ, EO, NZ * PCAP, dtype=f32)],
        )(here, *blocks)

    sent = call(
        back_kernel, "back", 60,
        in_specs=[SMEM] + [VMEM] * 3, out_specs=VMEM, out_shape=shape(NSRC, BROWS, 128),
        scratch_shapes=[
            pltpu.VMEM((DP, NY, NZ * 8, DZ), bf16),
            pltpu.VMEM((NZ, 16, DZ), f32),
        ],
    )(here, own, mine, other)
    back = lax.all_to_all(sent, "expert", 0, 0, tiled=True)

    own, sent = lax.optimization_barrier((own, sent))

    def over_z(v, k):
        pairs = [(a * NZ + b, a * NZ + (b + k) % NZ) for a in range(NY) for b in range(NZ)]
        return lax.ppermute(v, "expert", pairs)

    part_own = gather(0, own)
    left0, right0, right1, part_own, *lows = lax.optimization_barrier(
        (left0, right0, right1, part_own, *lows)
    )
    far0, far1 = over_y(left0, 1), over_y(right1, NY - 1)
    lows = [lows[0], over_z(lows[0], 3), over_z(lows[1], NZ - 3)]
    part_right = gather(80, right0, right1)
    left1, part_right = lax.optimization_barrier((left1, part_right))
    part_left = gather(0, left0, left1)
    back, part_right, part_left = lax.optimization_barrier((back, part_right, part_left))
    slots, big_a, sq_a = call(
        a_kernel, "norm_a", 0,
        grid=(EO,),
        in_specs=[
            whole(NSRC, BROWS, 128),
            pl.BlockSpec((1, SLOTS, F), lambda i: (i, 0, 0)),
        ],
        out_specs=[
            pl.BlockSpec((1, R, SLOTS), lambda i: (i, 0, 0)),
            pl.BlockSpec((1, NEX * R, F), lambda i: (i, 0, 0)),
            whole(NEX * R, 128),
        ],
        out_shape=[
            shape(EO, R, SLOTS),
            shape(EO, NEX * R, F),
            shape(NEX * R, 128, dtype=f32),
        ],
        scratch_shapes=[pltpu.VMEM((2 * R, NSRC * 64), bf16)],
    )(back, hidden)

    far0, far1, sq_a = lax.optimization_barrier((far0, far1, sq_a))
    parts = [part_own, part_right, gather(0, far0, far1, space=pltpu.VMEM), part_left]
    big_b, norm = call(
        b_kernel, "norm_b",
        grid=(NZ,),
        in_specs=[SMEM]
        + [pl.BlockSpec((EO, NZ * PCAP, DZ), lambda i: (i, 0, 0))] * 4
        + [pl.BlockSpec((1, EO, NZ * PCAP), lambda i: (i, 0, 0))] * 4
        + [
            *[whole(len(v) * EO * R, PSLOTS) for v in LOWS],
            whole(NEX * R, 128),
        ],
        out_specs=[
            pl.BlockSpec((EO, NEX * R, DZ), lambda i: (i, 0, 0)),
            whole(NSRC, 128),
        ],
        out_shape=[shape(EY, NEX * R, DZ), shape(NSRC, 128, dtype=f32)],
        scratch_shapes=[
            pltpu.VMEM((NEX * R, 128), f32),
            pltpu.VMEM((NZ, EO * R, PSLOTS), bf16),
        ],
    )(here, *[
            pltpu.with_memory_space_constraint(v[0], pltpu.VMEM) if n == 2 else v[0]
            for n, v in enumerate(parts)
        ], *[v[1] for v in parts], *lows, sq_a)
    norm = lax.all_to_all(norm, "expert", 0, 0, tiled=True)

    sums = call(
        clip_kernel, "clip",
        grid=(NZ,),
        in_specs=[
            whole(NSRC, 128),
            pl.BlockSpec((EO, NEX * R, DZ), lambda i: (i, 0, 0)),
            whole(EO, NEX * R, F),
        ],
        out_specs=whole(DP, EO * R, DZ + FA),
        out_shape=shape(DP, EO * R, DZ + FA),
        scratch_shapes=[pltpu.VMEM((EO * R, F), f32)],
    )(norm, big_b, big_a)
    slots, sums = lax.optimization_barrier((slots, sums))
    sums = lax.all_to_all(sums, "dp", 0, 0, tiled=True)
    hidden_grad = call(
        hidden_kernel, "hidden_grad",
        grid=(EO,),
        in_specs=[
            pl.BlockSpec((1, R, SLOTS), lambda i: (i, 0, 0)),
            pl.BlockSpec((1, R, F), lambda i: (i, 0, 0)),
        ],
        out_specs=pl.BlockSpec((1, SLOTS, F), lambda i: (i, 0, 0)),
        out_shape=shape(EO, SLOTS, F),
    )(slots, down)
    sums, hidden_grad = lax.optimization_barrier((sums, hidden_grad))
    sums = jnp.sum(sums.astype(f32), axis=0)
    swap = [
        ((g * NY + a) * NZ + b, (b * NY + a) * NZ + g)
        for g in range(DP) for a in range(NY) for b in range(NZ)
    ]
    grad_b = lax.ppermute(sums[:, :DZ].astype(bf16), ("dp", "expert"), swap).astype(f32)
    return (
        hidden_grad[None],
        sums[:, DZ:].reshape(EO, R, FA),
        grad_b.reshape(EO, R, DZ),
    )


def solution(mesh):
    return jax.shard_map(
        shards,
        mesh=mesh,
        in_specs=(
            P("dp", "expert", None),
            P("dp", "expert", None),
            P("dp", "expert", None),
            P("dp", "expert"),
            P("dp", "expert", None, None),
            P("expert", None, None),
            P("expert", None, None),
        ),
        out_specs=(P("dp", "expert", None, None), P("expert", None, "dp"), P("expert", None, "dp")),
        check_vma=False,
    )
```
